512 devices in a mesh: src: 32 (over x, y, core), tgt: 16 (over z).
Axes of the slice: x: 4, y: 4, z: 16, core: 2. Of those that a mesh axis runs over, the one named last changes fastest.
Arguments:
- sources: float32 [65536, 128], P('src'), may hold values from -3 to 3
- targets: float32 [16384, 128], P('tgt'), may hold values from -3 to 3
- log_source: float32 [65536], P('src'), may hold values from -1 to 1
- log_target: float32 [16384], P('tgt'), may hold values from -1 to 1
Outputs:
- source_potential: float32 [65536], P('src')
- target_potential: float32 [16384], P('tgt')
- barycentric: float32 [65536, 128], P('src')
The draws below stay inside these ranges and needn't reach their ends.
All inputs are finite; a program needn't handle non-finite values.
Results may differ from the reference program's by a relative error of at most 0.0003.
Values sent between devices are 32-bit elements; how exact they have to be, the bound alone decides.
A program may use at most 64 MiB of HBM per device.

```python
import math
import jax
import jax.numpy as jnp
from jax import lax

LATENT = 128
ITERS = 2
NS = 65536
NT = 16384


def latent_pair(key, src_lo, src_hi):
    keys = jax.random.split(key, 7)
    tgt_normal = jnp.clip(jax.random.normal(keys[0], (NT, LATENT), jnp.float32), -4.0, 4.0)
    tgt_scale = jnp.exp(jax.random.uniform(keys[2], (NT, 1), jnp.float32, jnp.log(0.7), jnp.log(1.4)))
    base = 0.5 * tgt_scale * tgt_normal
    paired = base.reshape(NT // 2, 2, LATENT)
    odd_rows = paired[:, 1, :]
    targets = jnp.stack([paired[:, 0, :], odd_rows], axis=1).reshape(NT, LATENT)
    src_normal = jnp.clip(jax.random.normal(keys[4], (NS, LATENT), jnp.float32), -4.0, 4.0)
    src_scale = jnp.exp(jax.random.uniform(keys[6], (NS, 1), jnp.float32, jnp.log(src_lo), jnp.log(src_hi)))
    sources = 0.5 * src_scale * src_normal
    return (sources, targets)


def draw_sources(key, part):
    pair = latent_pair(key, 0.7, 1.4)
    return pair[0]


def draw_targets(key, part):
    pair = latent_pair(key, 0.7, 1.4)
    return pair[1]


def block_levels(rng, dims, cuts, smallest, largest):
    factor_of = 1.0
    for dim, blocks in cuts:
        steps = jax.random.uniform(jax.random.fold_in(jax.random.fold_in(rng, 6), dim), (blocks,), jnp.float32, smallest / len(cuts), largest / len(cuts))
        factor_of = factor_of * jnp.repeat(jnp.exp(steps), dims[dim] // blocks).reshape((-1,) + (1,) * (len(dims) - 1 - dim))
    return factor_of


def setup_inputs(seed: int = 0) -> dict:
    key_of = jax.random.split(jax.random.key(seed), 5)
    sources = draw_sources(jax.random.fold_in(key_of[4], 71), 0)
    targets = draw_targets(jax.random.fold_in(key_of[4], 71), 0)
    log_source = jnp.clip(jax.random.uniform(key_of[2], (NS,), jnp.float32, -1.0, 1.0) * block_levels(key_of[2], (NS,), ((0, 32),), -0.4, 0.0), -1.0, 1.0)
    log_target = jnp.clip(jax.random.uniform(key_of[3], (NT,), jnp.float32, -1.0, 1.0) * block_levels(key_of[3], (NT,), ((0, 16),), -0.4, 0.0), -1.0, 1.0)
    return dict(sources=sources, targets=targets, log_source=log_source, log_target=log_target)


EPSILON = 1.0


def pair_cost(src_rows, targets, tgt_norms):
    src_norms = jnp.sum(src_rows * src_rows, axis=1)
    inner = jnp.dot(src_rows, targets.T, precision=lax.Precision.HIGHEST, preferred_element_type=jnp.float32)
    return (src_norms[:, None] + tgt_norms[None, :]) - 2.0 * inner


def reference(sources, targets, log_source, log_target):
    block_rows = math.gcd(NS, 1024)
    num_blocks = NS // block_rows
    src_blocks = sources.reshape(num_blocks, block_rows, LATENT)
    log_blocks = log_source.reshape(num_blocks, block_rows)
    tgt_norms = jnp.sum(targets * targets, axis=1)

    def row_step(target_pot):
        def block_row(pieces):
            src_rows, log_rows = pieces
            scores = (target_pot[None, :] - pair_cost(src_rows, targets, tgt_norms)) / EPSILON
            top_score = jnp.max(scores, axis=1)
            exp_total = jnp.sum(jnp.exp(scores - top_score[:, None]), axis=1)
            return EPSILON * log_rows - EPSILON * (top_score + jnp.log(exp_total))
        return lax.map(block_row, (src_blocks, log_blocks)).reshape(NS)

    def column_step(source_pot):
        pot_blocks = source_pot.reshape(num_blocks, block_rows)

        def block_col(state_pair, pieces):
            top_score, exp_total = state_pair
            src_rows, pot_rows = pieces
            scores = (pot_rows[:, None] - pair_cost(src_rows, targets, tgt_norms)) / EPSILON
            fresh_peak = jnp.maximum(top_score, jnp.max(scores, axis=0))
            exp_total = exp_total * jnp.exp(top_score - fresh_peak) + jnp.sum(jnp.exp(scores - fresh_peak[None, :]), axis=0)
            return (fresh_peak, exp_total), None

        start_state = (jnp.full((NT,), -jnp.inf, jnp.float32), jnp.zeros((NT,), jnp.float32))
        (top_score, exp_total), outcome = lax.scan(block_col, start_state, (src_blocks, pot_blocks))
        return EPSILON * log_target - EPSILON * (top_score + jnp.log(exp_total))

    target_pot = jnp.zeros((NT,), jnp.float32)
    source_pot = jnp.zeros((NS,), jnp.float32)
    for repeat in range(ITERS):
        source_pot = row_step(target_pot)
        target_pot = column_step(source_pot)

    def block_bary(src_rows):
        scores = (target_pot[None, :] - pair_cost(src_rows, targets, tgt_norms)) / EPSILON
        top_score = jnp.max(scores, axis=1)
        weights = jnp.exp(scores - top_score[:, None])
        weighted = jnp.dot(weights, targets, precision=lax.Precision.HIGHEST, preferred_element_type=jnp.float32)
        return weighted / jnp.sum(weights, axis=1)[:, None]

    barycentric = lax.map(block_bary, src_blocks).reshape(NS, LATENT)
    return source_pot, target_pot, barycentric
```

```python
import math

import jax
import jax.numpy as jnp
from jax import lax
from jax.experimental import pallas as pl
from jax.experimental.pallas import tpu as pltpu
from jax.sharding import PartitionSpec as P

ITERS = 2
LATENT = 128
LANES = 128
LOG2E = math.log2(math.e)
LN2 = math.log(2.0)
MESH = pl.DeviceIdType.MESH

NSRC, NTGT = 32, 16
GRID_X, GRID_Y = 4, 4
ROWS, COLS = 2048, 1024
RCH, CCH = ROWS // LANES, COLS // LANES
OWN = ROWS // NTGT
HALF = COLS // 2
PIECE = HALF // 8
F32, BF16 = jnp.float32, jnp.bfloat16


def split3(v, order):
    high = v.astype(BF16)
    low = (v - high.astype(F32)).astype(BF16)
    return jnp.concatenate([(high, low)[k] for k in order], axis=1)


def nt_dot(a, b):
    return lax.dot_general(a, b, (((1,), (1,)), ((), ())), preferred_element_type=F32)


def spread(row):
    return jnp.broadcast_to(row, (LANES, LANES)).T


def lse_pass(z_ref, b_ref, rows, cols, put):
    width, depth = 4, 64

    def load(block, col, k):
        at = pl.ds(pl.multiple_of(block * depth, depth), depth)
        lane = pl.multiple_of(col * width * LANES + k * LANES, LANES)
        return (z_ref[at, pl.ds(lane, LANES)] + b_ref[at, :]).reshape(depth // 8, 8, LANES)

    @pl.loop(0, cols // (width * LANES))
    def _(col):
        def top(block, acc):
            return tuple(jnp.maximum(acc[k], jnp.max(load(block, col, k), axis=0)) for k in range(width))

        start = tuple(jnp.full((8, LANES), -jnp.inf, F32) for _ in range(width))
        tops = lax.fori_loop(0, rows // depth, top, start)
        tops = [jnp.max(v, axis=0, keepdims=True) for v in tops]

        def total(block, acc):
            return tuple(
                acc[k] + jnp.sum(jnp.exp2(load(block, col, k) - tops[k].reshape(1, 1, LANES)), axis=0)
                for k in range(width)
            )

        sums = lax.fori_loop(0, rows // depth, total, tuple(jnp.zeros((8, LANES), F32) for _ in range(width)))
        for k in range(width):
            put(col * width + k, tops[k] + LOG2E * jnp.log(jnp.sum(sums[k], axis=0, keepdims=True)))


def combine(parts):
    top = jnp.max(parts, axis=0)
    return top + LOG2E * jnp.log(jnp.sum(jnp.exp2(parts - top[None]), axis=0))


def kernel(
    x_ref, y_ref, la_ref, lb_ref, sp_ref, tp_ref, out_ref,
    xa, ya, zt, z, qb, pb, nx, ny,
    l_row, rs, pg, l_col, cr, qs, qg, tg, xs, yf, zf, mf, sf, acc, part, sib,
    rs_send, rs_recv, pg_send, pg_recv, cr_send, cr_recv, qg_send, qg_recv,
    tr_send, tr_recv, plane_send, plane_recv, or_send, or_recv, xs_sem, sib_sem,
):
    s, t = lax.axis_index("src"), lax.axis_index("tgt")
    gx, gy, core = s // (GRID_Y * 2), lax.rem(s // 2, GRID_Y), lax.rem(s, 2)
    mate = s + 1 - 2 * core

    def z_peer(k):
        return lax.rem(t + k, NTGT)

    def s_peer(k):
        return lax.rem(s + k, NSRC)

    barrier = pltpu.get_barrier_semaphore()

    @pl.loop(1, NTGT)
    def _(k):
        pl.semaphore_signal(barrier, inc=1, device_id=(s, z_peer(k)), device_id_type=MESH)

    @pl.loop(1, NSRC)
    def _(k):
        pl.semaphore_signal(barrier, inc=1, device_id=(s_peer(k), t), device_id_type=MESH)

    def remote(src, dst, send, recv, device):
        return pltpu.make_async_remote_copy(
            src_ref=src, dst_ref=dst, send_sem=send, recv_sem=recv, device_id=device, device_id_type=MESH
        )

    @pl.loop(0, ROWS // 256)
    def _(k):
        at = pl.ds(pl.multiple_of(k * 256, 256), 256)
        xa[at, :] = split3(x_ref[at, :] * (2.0 * LOG2E), (0, 0, 1))

    @pl.loop(0, COLS // 256)
    def _(k):
        at = pl.ds(pl.multiple_of(k * 256, 256), 256)
        y = y_ref[at, :]
        ya[at, :] = split3(y, (0, 1, 0))
        qb[at, :] = jnp.broadcast_to(-LOG2E * jnp.sum(y * y, axis=1, keepdims=True), (256, LANES))

    slots = (gx, GRID_X + gy)
    for slot in slots:
        tg[slot, t] = y_ref[pl.ds(pl.multiple_of(core * HALF + slot * PIECE, PIECE), PIECE), :]
    own_rows = pl.ds(pl.multiple_of(t * OWN, OWN), OWN)
    xs[core] = x_ref[own_rows, :]

    pl.semaphore_wait(barrier, NTGT - 1 + NSRC - 1)

    def hops(way, chunk):
        return NTGT // 2 - (way ^ chunk)

    def ring_copy(view, send, recv, way, chunk, step):
        block = lax.rem(t + NTGT - step, NTGT) if way == 0 else lax.rem(t + step, NTGT)
        to = lax.rem(t + 1, NTGT) if way == 0 else lax.rem(t + NTGT - 1, NTGT)
        ref = view(chunk, block)
        return remote(ref, ref, send.at[way, chunk, step], recv.at[way, chunk, step], (s, to)), block

    def ring_arrival(view, send, recv, way, chunk, step):
        block = lax.rem(t + NTGT - step, NTGT) if way == 0 else lax.rem(t + step, NTGT)
        ref = view(chunk, block)
        remote(ref, ref, send.at[way, chunk, step - 1], recv.at[way, chunk, step - 1], (s, t)).wait_recv()
        return block

    def ring_step(view, send, recv, step, then=None):
        for chunk in range(2):
            for way in range(2):
                if step > hops(way, chunk):
                    continue
                block = t
                if step > 0:
                    block = ring_arrival(view, send, recv, way, chunk, step)
                if step < hops(way, chunk):
                    ring_copy(view, send, recv, way, chunk, step)[0].start()
                if then is not None and (step > 0 or way == 0):
                    then(chunk, block)

    def ring_drain(view, send, recv):
        for chunk in range(2):
            for way in range(2):
                for step in range(hops(way, chunk)):
                    ring_copy(view, send, recv, way, chunk, step)[0].wait_send()

    def plane_peer(chunk, k):
        if chunk == 0:
            return lax.rem(s + k * GRID_Y * 2, NSRC)
        return (gx * GRID_Y + lax.rem(gy + k, GRID_Y)) * 2 + core

    def plane_copy(chunk, k, ref):
        return remote(
            ref, ref, plane_send.at[chunk, k - 1], plane_recv.at[slots[chunk]], (plane_peer(chunk, k), t)
        )

    def to_plane(chunk, block):
        for k in range(1, 4):
            plane_copy(chunk, k, tg.at[slots[chunk], block]).start()

    def t_view(chunk, block):
        return tg.at[slots[chunk], block]

    def t_step(step):
        ring_step(t_view, tr_send, tr_recv, step, to_plane)

    def xs_copy():
        return remote(xs.at[core], xs.at[core], xs_sem.at[0], xs_sem.at[1], (mate, t))

    t_step(0)
    xs_copy().start()

    @pl.loop(0, ROWS // 256)
    def _(k):
        at = pl.ds(pl.multiple_of(k * 256, 256), 256)
        zt[:, at] = nt_dot(ya[...], xa[at, :])

    t_step(1)

    def row_copy(it, k):
        to = z_peer(k)
        return remote(l_row.at[it, to], rs.at[it, t], rs_send.at[it, to], rs_recv.at[it, t], (s, to))

    def pot_copy(it, k):
        to = z_peer(k)
        return remote(pg.at[it, t], pg.at[it, t], pg_send.at[it, to], pg_recv.at[it, t], (s, to))

    def col_copy(it, k):
        to = s_peer(k)
        return remote(l_col.at[it], cr.at[it, s], cr_send.at[it, to], cr_recv.at[it, s], (to, t))

    def last_copy(k):
        to = z_peer(k)
        return remote(qs.at[core], qg.at[t], qg_send.at[to], qg_recv.at[t], (s, to))

    for it in range(ITERS):

        def put_row(chunk, value):
            l_row[it, chunk] = value

        lse_pass(zt, qb, COLS, ROWS, put_row)
        rs[it, t] = l_row[it, t]

        @pl.loop(1, NTGT)
        def _(k):
            row_copy(it, k).start()

        if it == 0:
            t_step(2)
            for half in range(2):
                @pl.loop(half * 2, half * 2 + 2)
                def _(k):
                    at = pl.ds(pl.multiple_of(k * 256, 256), 256)
                    z[:, at] = nt_dot(xa[...], ya[at, :])

                if half == 0:
                    t_step(3)
        else:
            t_step(7)

        @pl.loop(1, NTGT)
        def _(k):
            frm = z_peer(k)
            remote(l_row.at[it, frm], rs.at[it, frm], rs_send.at[it, frm], rs_recv.at[it, frm], (s, frm)).wait_recv()

        pg[it, t] = LOG2E * la_ref[t] - combine(rs[it])

        @pl.loop(1, NTGT)
        def _(k):
            pot_copy(it, k).start()

        if it == 0:
            t_step(4)

            @pl.loop(0, RCH)
            def _(k):
                block = x_ref[pl.ds(pl.multiple_of(k * LANES, LANES), LANES), :]
                nx[k] = jnp.sum((block * block).T, axis=0, keepdims=True)

            for k in range(CCH):
                ny[k : k + 1, :] = qb[k * LANES : (k + 1) * LANES, :].T[0:1, :] * (-LN2)
        else:
            t_step(8)

        @pl.loop(1, NTGT)
        def _(k):
            frm = z_peer(k)
            remote(pg.at[it, frm], pg.at[it, frm], pg_send.at[it, frm], pg_recv.at[it, frm], (s, frm)).wait_recv()

        @pl.loop(0, RCH)
        def _(k):
            pb[pl.ds(pl.multiple_of(k * LANES, LANES), LANES), :] = spread(pg[it, k])

        def put_col(chunk, value):
            l_col[it, pl.ds(chunk, 1), :] = value

        lse_pass(z, pb, ROWS, COLS, put_col)

        @pl.loop(1, NSRC)
        def _(k):
            col_copy(it, k).start()

        cr[it, s] = l_col[it]
        if it == 0:
            t_step(5)
        else:
            sp_ref[...] = pg[it] * LN2 + nx[...]
            for slot in range(8):
                chunk, place = slot // 4, slot % 4

                @pl.when(slot != slots[chunk])
                def _():
                    remote(
                        tg.at[slot], tg.at[slot], plane_send.at[chunk, 0], plane_recv.at[slot], (s, t)
                    ).wait_recv()

            xs_mine = xs.at[1 - core]
            remote(xs_mine, xs_mine, xs_sem.at[0], xs_sem.at[1], (mate, t)).wait_recv()
            xf = split3(xs[...].reshape(2 * OWN, LATENT) * (2.0 * LOG2E), (0, 0, 1))
            xa[0 : 2 * OWN, :] = xf

            @pl.loop(0, NTGT)
            def _(b):
                at = pl.ds(pl.multiple_of(b * HALF, HALF), HALF)
                yf[at, :] = split3(tg[:, b].reshape(HALF, LATENT), (0, 1, 0))
                zf[:, at] = nt_dot(xa[0 : 2 * OWN, :], yf[at, :])

        @pl.loop(1, NSRC)
        def _(k):
            frm = s_peer(k)
            remote(l_col.at[it], cr.at[it, frm], cr_send.at[it, frm], cr_recv.at[it, frm], (frm, t)).wait_recv()

        q = LOG2E * lb_ref[...] - combine(cr[it])
        if it == 0:
            for k in range(CCH):
                qb[k * LANES : (k + 1) * LANES, :] = spread(q[k : k + 1, :])
            t_step(6)

    qs[0] = q[0 : CCH // 2, :]
    qs[1] = q[CCH // 2 :, :]
    qg[t] = qs[core]

    @pl.loop(1, NTGT)
    def _(k):
        last_copy(k).start()

    tp_ref[...] = q * LN2 + ny[...]

    @pl.loop(1, NTGT)
    def _(k):
        frm = z_peer(k)
        remote(qs.at[core], qg.at[frm], qg_send.at[frm], qg_recv.at[frm], (s, frm)).wait_recv()

    depth = 64

    @pl.loop(0, 2 * OWN // depth)
    def _(r):
        at = pl.ds(pl.multiple_of(r * depth, depth), depth)

        def top(b, best):
            for k in range(HALF // LANES):
                lane = pl.ds(pl.multiple_of(b * HALF + k * LANES, LANES), LANES)
                best = jnp.maximum(best, zf[at, lane] + qg[b, k : k + 1, :])
            return best

        best = lax.fori_loop(0, NTGT, top, jnp.full((depth, LANES), -jnp.inf, F32))
        mf[at, :] = jnp.broadcast_to(jnp.max(best, axis=1, keepdims=True), (depth, LANES))

    sf[...] = jnp.zeros_like(sf)
    acc[...] = jnp.zeros_like(acc)

    @pl.loop(0, NTGT)
    def _(b):
        highs, lows = [], []
        total = sf[...]
        for k in range(HALF // LANES):
            lane = pl.ds(pl.multiple_of(b * HALF + k * LANES, LANES), LANES)
            w = jnp.exp2(zf[:, lane] + qg[b, k : k + 1, :] - mf[...])
            total += w
            high = w.astype(BF16)
            highs.append(high)
            lows.append((w - high.astype(F32)).astype(BF16))
        sf[...] = total
        at = pl.ds(pl.multiple_of(b * HALF, HALF), HALF)
        both = jnp.dot(jnp.concatenate(highs, axis=1), yf[at, 0 : 2 * LATENT], preferred_element_type=F32)
        rest = jnp.dot(jnp.concatenate(lows, axis=1), yf[at, 0:LATENT], preferred_element_type=F32)
        acc[...] += both[:, :LATENT] + both[:, LATENT:] + rest

    left = lax.broadcasted_iota(jnp.int32, (OWN, LANES), 1) < LANES // 2
    for g in range(2):
        at = slice(g * OWN, (g + 1) * OWN)
        part[g, 0] = acc[at, :]
        part[g, 1] = jnp.where(left, mf[at, :], jnp.sum(sf[at, :], axis=1, keepdims=True))

    def sib_copy():
        return remote(part.at[1 - core], sib, sib_sem.at[0], sib_sem.at[1], (mate, t))

    sib_copy().start()
    mine, mine_stat = part[core, 0], part[core, 1]
    sib_copy().wait_recv()
    m0, s0 = mine_stat[:, 0:1], mine_stat[:, LANES // 2 : LANES // 2 + 1]
    m1, s1 = sib[1, :, 0:1], sib[1, :, LANES // 2 : LANES // 2 + 1]
    best = jnp.maximum(m0, m1)
    e0, e1 = jnp.exp2(m0 - best), jnp.exp2(m1 - best)
    out_ref[own_rows, :] = (e0 * mine + e1 * sib[0]) / (e0 * s0 + e1 * s1)

    def o_view(chunk, block):
        rows = OWN // 2
        return out_ref.at[pl.ds(pl.multiple_of(block * OWN + chunk * rows, rows), rows), :]

    for step in range(NTGT // 2 + 1):
        ring_step(o_view, or_send, or_recv, step)

    ring_drain(t_view, tr_send, tr_recv)
    ring_drain(o_view, or_send, or_recv)
    for chunk in range(2):
        for k in range(1, 4):
            plane_copy(chunk, k, tg.at[slots[chunk]]).wait_send()
    xs_copy().wait_send()
    sib_copy().wait_send()
    for it in range(ITERS):

        @pl.loop(1, NTGT)
        def _(k):
            row_copy(it, k).wait_send()
            pot_copy(it, k).wait_send()

        @pl.loop(1, NSRC)
        def _(k):
            col_copy(it, k).wait_send()

    @pl.loop(1, NTGT)
    def _(k):
        last_copy(k).wait_send()


def on_device(sources, targets, log_source, log_target):
    vmem = pl.BlockSpec(memory_space=pltpu.VMEM)
    dma = pltpu.SemaphoreType.DMA
    sp, tp, bary = pl.pallas_call(
        kernel,
        out_shape=(
            jax.ShapeDtypeStruct((RCH, 1, LANES), F32),
            jax.ShapeDtypeStruct((CCH, LANES), F32),
            jax.ShapeDtypeStruct((ROWS, LATENT), F32),
        ),
        in_specs=[vmem] * 4,
        out_specs=(vmem,) * 3,
        scratch_shapes=[
            pltpu.VMEM((ROWS, 3 * LATENT), BF16),
            pltpu.VMEM((COLS, 3 * LATENT), BF16),
            pltpu.VMEM((COLS, ROWS), F32),
            pltpu.VMEM((ROWS, COLS), F32),
            pltpu.VMEM((COLS, LANES), F32),
            pltpu.VMEM((ROWS, LANES), F32),
            pltpu.VMEM((RCH, 1, LANES), F32),
            pltpu.VMEM((CCH, LANES), F32),
            pltpu.VMEM((ITERS, RCH, 1, LANES), F32),
            pltpu.VMEM((ITERS, NTGT, 1, LANES), F32),
            pltpu.VMEM((ITERS, RCH, 1, LANES), F32),
            pltpu.VMEM((ITERS, CCH, LANES), F32),
            pltpu.VMEM((ITERS, NSRC, CCH, LANES), F32),
            pltpu.VMEM((2, CCH // 2, LANES), F32),
            pltpu.VMEM((NTGT, CCH // 2, LANES), F32),
            pltpu.VMEM((8, NTGT, PIECE, LATENT), F32),
            pltpu.VMEM((2, OWN, LATENT), F32),
            pltpu.VMEM((NTGT * HALF, 3 * LATENT), BF16),
            pltpu.VMEM((2 * OWN, NTGT * HALF), F32),
            pltpu.VMEM((2 * OWN, LANES), F32),
            pltpu.VMEM((2 * OWN, LANES), F32),
            pltpu.VMEM((2 * OWN, LATENT), F32),
            pltpu.VMEM((2, 2, OWN, LATENT), F32),
            pltpu.VMEM((2, OWN, LATENT), F32),
            dma((ITERS, NTGT)), dma((ITERS, NTGT)),
            dma((ITERS, NTGT)), dma((ITERS, NTGT)),
            dma((ITERS, NSRC)), dma((ITERS, NSRC)),
            dma((NTGT,)), dma((NTGT,)),
            dma((2, 2, 8)), dma((2, 2, 8)),
            dma((2, 3)), dma((8,)),
            dma((2, 2, 8)), dma((2, 2, 8)),
            dma((2,)),
            dma((2,)),
        ],
        compiler_params=pltpu.CompilerParams(
            collective_id=0, has_side_effects=True, vmem_limit_bytes=56 * 2**20
        ),
        cost_estimate=pl.CostEstimate(flops=6 * 10**9, bytes_accessed=4 * 2**20, transcendentals=10**7),
        name="coupling",
    )(
        sources,
        targets,
        log_source.reshape(RCH, 1, LANES),
        log_target.reshape(CCH, LANES),
    )
    return sp.reshape(ROWS), tp.reshape(COLS), bary


def solution(mesh):
    in_specs = (P("src", None), P("tgt", None), P("src"), P("tgt"))
    out_specs = (P("src"), P("tgt"), P("src", None))
    return jax.shard_map(
        on_device, mesh=mesh, in_specs=in_specs, out_specs=out_specs, check_vma=False
    )
```

```python
import math

import jax
import jax.numpy as jnp
from jax import lax
from jax.experimental import pallas as pl
from jax.experimental.pallas import tpu as pltpu
from jax.sharding import PartitionSpec as P

ITERS = 2
LATENT = 128
LANES = 128
LOG2E = math.log2(math.e)
LN2 = math.log(2.0)
MESH = pl.DeviceIdType.MESH

NSRC, NTGT = 32, 16
GRID_X, GRID_Y = 4, 4
ROWS, COLS = 2048, 1024
RCH, CCH = ROWS // LANES, COLS // LANES
OWN = ROWS // NTGT
MATES = GRID_X * 2
PIECE = COLS // MATES
F32, BF16 = jnp.float32, jnp.bfloat16


def split3(v, order):
    high = v.astype(BF16)
    low = (v - high.astype(F32)).astype(BF16)
    return jnp.concatenate([(high, low)[k] for k in order], axis=1)


def nt_dot(a, b):
    return lax.dot_general(a, b, (((1,), (1,)), ((), ())), preferred_element_type=F32)


def spread(row):
    return jnp.broadcast_to(row, (LANES, LANES)).T


def lse_pass(z_ref, b_ref, rows, cols, put):
    width, depth = 4, 64

    def load(block, col, k):
        at = pl.ds(pl.multiple_of(block * depth, depth), depth)
        lane = pl.multiple_of(col * width * LANES + k * LANES, LANES)
        return (z_ref[at, pl.ds(lane, LANES)] + b_ref[at, :]).reshape(depth // 8, 8, LANES)

    @pl.loop(0, cols // (width * LANES))
    def _(col):
        def top(block, acc):
            return tuple(jnp.maximum(acc[k], jnp.max(load(block, col, k), axis=0)) for k in range(width))

        start = tuple(jnp.full((8, LANES), -jnp.inf, F32) for _ in range(width))
        tops = lax.fori_loop(0, rows // depth, top, start)
        tops = [jnp.max(v, axis=0, keepdims=True) for v in tops]

        def total(block, acc):
            return tuple(
                acc[k] + jnp.sum(jnp.exp2(load(block, col, k) - tops[k].reshape(1, 1, LANES)), axis=0)
                for k in range(width)
            )

        sums = lax.fori_loop(0, rows // depth, total, tuple(jnp.zeros((8, LANES), F32) for _ in range(width)))
        for k in range(width):
            put(col * width + k, tops[k] + LOG2E * jnp.log(jnp.sum(sums[k], axis=0, keepdims=True)))


def combine(parts):
    top = jnp.max(parts, axis=0)
    return top + LOG2E * jnp.log(jnp.sum(jnp.exp2(parts - top[None]), axis=0))


def kernel(
    x_ref, y_ref, la_ref, lb_ref, sp_ref, tp_ref, out_ref,
    xa, ya, zt, z, qb, pb, nx, ny,
    l_row, rs, pg, l_col, cr, qs, qg, tg, xs, xf, yf, mf, sf, acc, part, shares,
    rs_sem, pg_sem, cr_sem, qg_sem, tr_send, tr_recv, or_send, or_recv, xs_sem, part_sem,
):
    s, t = lax.axis_index("src"), lax.axis_index("tgt")
    gx, gy, core = s // (GRID_Y * 2), lax.rem(s // 2, GRID_Y), lax.rem(s, 2)
    me = gx * 2 + core

    def z_peer(k):
        return lax.rem(t + k, NTGT)

    def s_peer(k):
        return lax.rem(s + k, NSRC)

    def mate(e):
        return ((e // 2) * GRID_Y + gy) * 2 + lax.rem(e, 2)

    barrier = pltpu.get_barrier_semaphore()

    @pl.loop(1, NTGT)
    def _(k):
        pl.semaphore_signal(barrier, inc=1, device_id=(s, z_peer(k)), device_id_type=MESH)

    @pl.loop(1, NSRC)
    def _(k):
        pl.semaphore_signal(barrier, inc=1, device_id=(s_peer(k), t), device_id_type=MESH)

    def remote(src, dst, send, recv, device):
        return pltpu.make_async_remote_copy(
            src_ref=src, dst_ref=dst, send_sem=send, recv_sem=recv, device_id=device, device_id_type=MESH
        )

    def wait_bytes(ref, sem):
        remote(ref, ref, sem, sem, (s, t)).wait_recv()

    @pl.loop(0, ROWS // 256)
    def _(k):
        at = pl.ds(pl.multiple_of(k * 256, 256), 256)
        xa[at, :] = split3(x_ref[at, :] * (2.0 * LOG2E), (0, 0, 1))

    @pl.loop(0, COLS // 256)
    def _(k):
        at = pl.ds(pl.multiple_of(k * 256, 256), 256)
        y = y_ref[at, :]
        ya[at, :] = split3(y, (0, 1, 0))
        qb[at, :] = jnp.broadcast_to(-LOG2E * jnp.sum(y * y, axis=1, keepdims=True), (256, LANES))

    tg[t] = y_ref[pl.ds(pl.multiple_of(me * PIECE, PIECE), PIECE), :]
    own_rows = pl.ds(pl.multiple_of(t * OWN, OWN), OWN)
    xs[me] = x_ref[own_rows, :]

    pl.semaphore_wait(barrier, NTGT - 1 + NSRC - 1)

    def hops(way, chunk):
        return NTGT // 2 - (way ^ chunk)

    def ring_step(view, send, recv, step):
        for chunk in range(2):
            for way in range(2):
                if step > hops(way, chunk):
                    continue
                block = lax.rem(t + (NTGT - step if way == 0 else step), NTGT)
                ref = view(chunk, block)
                if step > 0:
                    wait_bytes(ref, recv.at[way, chunk, step - 1])
                if step < hops(way, chunk):
                    to = lax.rem(t + (1 if way == 0 else NTGT - 1), NTGT)
                    remote(ref, ref, send.at[way, chunk], recv.at[way, chunk, step], (s, to)).start()

    def t_view(chunk, block):
        return tg.at[block, pl.ds(chunk * (PIECE // 2), PIECE // 2), :]

    def t_step(step):
        ring_step(t_view, tr_send, tr_recv, step)

    t_step(0)

    @pl.loop(1, MATES)
    def _(k):
        to = mate(lax.rem(me + k, MATES))
        remote(xs.at[me], xs.at[me], xs_sem.at[0], xs_sem.at[1], (to, t)).start()

    @pl.loop(0, ROWS // 256)
    def _(k):
        at = pl.ds(pl.multiple_of(k * 256, 256), 256)
        zt[:, at] = nt_dot(ya[...], xa[at, :])

    t_step(1)

    for it in range(ITERS):

        def put_row(chunk, value):
            l_row[it, chunk] = value

        lse_pass(zt, qb, COLS, ROWS, put_row)
        rs[it, t] = l_row[it, t]

        @pl.loop(1, NTGT)
        def _(k):
            to = z_peer(k)
            remote(l_row.at[it, to], rs.at[it, t], rs_sem.at[it, 0], rs_sem.at[it, 1], (s, to)).start()

        if it == 0:
            t_step(2)
            for half in range(2):
                @pl.loop(half * 2, half * 2 + 2)
                def _(k):
                    at = pl.ds(pl.multiple_of(k * 256, 256), 256)
                    z[:, at] = nt_dot(xa[...], ya[at, :])

                if half == 0:
                    t_step(3)
        else:
            t_step(7)

        wait_bytes(rs.at[it, pl.ds(0, NTGT - 1)], rs_sem.at[it, 1])
        pg[it, t] = LOG2E * la_ref[t] - combine(rs[it])

        @pl.loop(1, NTGT)
        def _(k):
            remote(pg.at[it, t], pg.at[it, t], pg_sem.at[it, 0], pg_sem.at[it, 1], (s, z_peer(k))).start()

        if it == 0:
            t_step(4)

            for k in range(RCH):
                block = x_ref[k * LANES : (k + 1) * LANES, :]
                nx[k] = jnp.sum((block * block).T, axis=0, keepdims=True)
            for k in range(CCH):
                ny[k : k + 1, :] = qb[k * LANES : (k + 1) * LANES, :].T[0:1, :] * (-LN2)
        else:
            t_step(8)

        wait_bytes(pg.at[it, pl.ds(0, NTGT - 1)], pg_sem.at[it, 1])
        for k in range(RCH):
            pb[k * LANES : (k + 1) * LANES, :] = spread(pg[it, k])

        def put_col(chunk, value):
            l_col[it, pl.ds(chunk, 1), :] = value

        lse_pass(z, pb, ROWS, COLS, put_col)

        @pl.loop(1, NSRC)
        def _(k):
            remote(l_col.at[it], cr.at[it, s], cr_sem.at[it, 0], cr_sem.at[it, 1], (s_peer(k), t)).start()

        cr[it, s] = l_col[it]
        if it == 0:
            t_step(5)
        else:
            sp_ref[...] = pg[it] * LN2 + nx[...]
            wait_bytes(xs.at[pl.ds(0, MATES - 1)], xs_sem.at[1])

            @pl.loop(0, MATES)
            def _(e):
                at = pl.ds(pl.multiple_of(e * OWN, OWN), OWN)
                xf[at, :] = split3(xs[e] * (2.0 * LOG2E), (0, 0, 1))

            @pl.loop(0, NTGT // 2)
            def _(b):
                at = pl.ds(pl.multiple_of(b * 2 * PIECE, 2 * PIECE), 2 * PIECE)
                yf[at, :] = split3(tg[pl.ds(b * 2, 2)].reshape(2 * PIECE, LATENT), (0, 1, 0))
                zt[:, at] = nt_dot(xf[...], yf[at, :])

        wait_bytes(cr.at[it, pl.ds(0, NSRC - 1)], cr_sem.at[it, 1])
        q = LOG2E * lb_ref[...] - combine(cr[it])
        if it == 0:
            for k in range(CCH):
                qb[k * LANES : (k + 1) * LANES, :] = spread(q[k : k + 1, :])
            t_step(6)

    for k in range(CCH):
        qs[k] = q[k : k + 1, :]
    qg[t] = qs[me]

    @pl.loop(1, NTGT)
    def _(k):
        remote(qs.at[me], qg.at[t], qg_sem.at[0], qg_sem.at[1], (s, z_peer(k))).start()

    tp_ref[...] = q * LN2 + ny[...]
    wait_bytes(qg.at[pl.ds(0, NTGT - 1)], qg_sem.at[1])

    depth = 64
    for far in (2, 1, 3, 0):
        chip = lax.rem(gx + far, GRID_X)
        base = chip * 2 * OWN

        @pl.loop(0, 2 * OWN // depth)
        def _(r):
            at = pl.ds(pl.multiple_of(base + r * depth, depth), depth)
            best = zt[at, 0:LANES] + qg[0]
            for b in range(1, NTGT):
                best = jnp.maximum(best, zt[at, b * LANES : (b + 1) * LANES] + qg[b])
            to = pl.ds(pl.multiple_of(r * depth, depth), depth)
            mf[to, :] = jnp.broadcast_to(jnp.max(best, axis=1, keepdims=True), (depth, LANES))

        sf[...] = jnp.zeros_like(sf)
        acc[...] = jnp.zeros_like(acc)
        at = pl.ds(pl.multiple_of(base, 2 * OWN), 2 * OWN)
        group = 4

        @pl.loop(0, NTGT // group)
        def _(b):
            highs, lows = [], []
            total = sf[...]
            for k in range(group):
                lane = pl.ds(pl.multiple_of((b * group + k) * LANES, LANES), LANES)
                w = jnp.exp2(zt[at, lane] + qg[b * group + k] - mf[...])
                total += w
                high = w.astype(BF16)
                highs.append(high)
                lows.append((w - high.astype(F32)).astype(BF16))
            sf[...] = total
            ys = pl.ds(pl.multiple_of(b * group * LANES, group * LANES), group * LANES)
            both = jnp.dot(jnp.concatenate(highs, axis=1), yf[ys, 0 : 2 * LATENT], preferred_element_type=F32)
            rest = jnp.dot(jnp.concatenate(lows, axis=1), yf[ys, 0:LATENT], preferred_element_type=F32)
            acc[...] += both[:, :LATENT] + both[:, LATENT:] + rest

        for g in range(2):
            rows = slice(g * OWN, (g + 1) * OWN)
            to = chip * 2 + g
            part[to, 0:OWN, :] = acc[rows, :]
            part[to, OWN : OWN + 1, :] = mf[rows, :].T[0:1, :]
            part[to, OWN + 1 : OWN + 2, :] = jnp.sum(sf[rows, :].T, axis=0, keepdims=True)

            def send():
                remote(part.at[to], shares.at[me], part_sem.at[0], part_sem.at[1], (mate(to), t)).start()

            if far == 0:
                pl.when(core != g)(send)
            else:
                send()

    shares[me, 0 : OWN + 2, :] = part[me, 0 : OWN + 2, :]
    wait_bytes(shares.at[pl.ds(0, MATES - 1)], part_sem.at[1])
    tops = [shares[e, OWN : OWN + 1, :] for e in range(MATES)]
    best = tops[0]
    for v in tops[1:]:
        best = jnp.maximum(best, v)
    scales = [jnp.exp2(v - best) for v in tops]
    total = sum(scales[e] * shares[e, OWN + 1 : OWN + 2, :] for e in range(MATES))
    out = jnp.zeros((OWN, LATENT), F32)
    for e in range(MATES):
        out += spread(scales[e] / total) * shares[e, 0:OWN, :]
    out_ref[own_rows, :] = out

    def o_view(chunk, block):
        rows = OWN // 2
        return out_ref.at[pl.ds(pl.multiple_of(block * OWN + chunk * rows, rows), rows), :]

    for step in range(NTGT // 2 + 1):
        ring_step(o_view, or_send, or_recv, step)

    for chunk in range(2):
        for way in range(2):
            n = hops(way, chunk)
            wait_bytes(tg.at[pl.ds(0, n), pl.ds(0, PIECE // 2), :], tr_send.at[way, chunk])
            wait_bytes(out_ref.at[pl.ds(0, n * (OWN // 2)), :], or_send.at[way, chunk])
    wait_bytes(xs.at[pl.ds(0, MATES - 1)], xs_sem.at[0])
    wait_bytes(part.at[pl.ds(0, MATES - 1)], part_sem.at[0])
    for it in range(ITERS):
        wait_bytes(rs.at[it, pl.ds(0, NTGT - 1)], rs_sem.at[it, 0])
        wait_bytes(pg.at[it, pl.ds(0, NTGT - 1)], pg_sem.at[it, 0])
        wait_bytes(cr.at[it, pl.ds(0, NSRC - 1)], cr_sem.at[it, 0])
    wait_bytes(qg.at[pl.ds(0, NTGT - 1)], qg_sem.at[0])


def on_device(sources, targets, log_source, log_target):
    vmem = pl.BlockSpec(memory_space=pltpu.VMEM)
    dma = pltpu.SemaphoreType.DMA
    sp, tp, bary = pl.pallas_call(
        kernel,
        out_shape=(
            jax.ShapeDtypeStruct((RCH, 1, LANES), F32),
            jax.ShapeDtypeStruct((CCH, LANES), F32),
            jax.ShapeDtypeStruct((ROWS, LATENT), F32),
        ),
        in_specs=[vmem] * 4,
        out_specs=(vmem,) * 3,
        scratch_shapes=[
            pltpu.VMEM((ROWS, 3 * LATENT), BF16),
            pltpu.VMEM((COLS, 3 * LATENT), BF16),
            pltpu.VMEM((COLS, ROWS), F32),
            pltpu.VMEM((ROWS, COLS), F32),
            pltpu.VMEM((COLS, LANES), F32),
            pltpu.VMEM((ROWS, LANES), F32),
            pltpu.VMEM((RCH, 1, LANES), F32),
            pltpu.VMEM((CCH, LANES), F32),
            pltpu.VMEM((ITERS, RCH, 1, LANES), F32),
            pltpu.VMEM((ITERS, NTGT, 1, LANES), F32),
            pltpu.VMEM((ITERS, RCH, 1, LANES), F32),
            pltpu.VMEM((ITERS, CCH, LANES), F32),
            pltpu.VMEM((ITERS, NSRC, CCH, LANES), F32),
            pltpu.VMEM((CCH, 1, LANES), F32),
            pltpu.VMEM((NTGT, 1, LANES), F32),
            pltpu.VMEM((NTGT, PIECE, LATENT), F32),
            pltpu.VMEM((MATES, OWN, LATENT), F32),
            pltpu.VMEM((MATES * OWN, 3 * LATENT), BF16),
            pltpu.VMEM((NTGT * PIECE, 3 * LATENT), BF16),
            pltpu.VMEM((2 * OWN, LANES), F32),
            pltpu.VMEM((2 * OWN, LANES), F32),
            pltpu.VMEM((2 * OWN, LATENT), F32),
            pltpu.VMEM((MATES, OWN + 8, LATENT), F32),
            pltpu.VMEM((MATES, OWN + 8, LATENT), F32),
            dma((ITERS, 2)),
            dma((ITERS, 2)),
            dma((ITERS, 2)),
            dma((2,)),
            dma((2, 2)), dma((2, 2, 8)),
            dma((2, 2)), dma((2, 2, 8)),
            dma((2,)),
            dma((2,)),
        ],
        compiler_params=pltpu.CompilerParams(
            collective_id=0, has_side_effects=True, vmem_limit_bytes=56 * 2**20
        ),
        cost_estimate=pl.CostEstimate(flops=6 * 10**9, bytes_accessed=4 * 2**20, transcendentals=10**7),
        name="coupling",
    )(
        sources,
        targets,
        log_source.reshape(RCH, 1, LANES),
        log_target.reshape(CCH, LANES),
    )
    return sp.reshape(ROWS), tp.reshape(COLS), bary


def solution(mesh):
    in_specs = (P("src", None), P("tgt", None), P("src"), P("tgt"))
    out_specs = (P("src"), P("tgt"), P("src", None))
    return jax.shard_map(
        on_device, mesh=mesh, in_specs=in_specs, out_specs=out_specs, check_vma=False
    )
```

```python
import math

import jax
import jax.numpy as jnp
from jax import lax
from jax.experimental import pallas as pl
from jax.experimental.pallas import tpu as pltpu
from jax.sharding import PartitionSpec as P

ITERS = 2
LATENT = 128
LANES = 128
LOG2E = math.log2(math.e)
LN2 = math.log(2.0)
MESH = pl.DeviceIdType.MESH

NSRC, NTGT = 32, 16
GRID_X, GRID_Y = 4, 4
ROWS, COLS = 2048, 1024
RCH, CCH = ROWS // LANES, COLS // LANES
OWN = ROWS // NTGT
MATES = GRID_X * 2
PIECE = COLS // MATES
F32, BF16 = jnp.float32, jnp.bfloat16


def split3(v, order, axis=1):
    high = v.astype(BF16)
    low = (v - high.astype(F32)).astype(BF16)
    return jnp.concatenate([(high, low)[k] for k in order], axis=axis)


def dot(a, b):
    return jnp.dot(a, b, preferred_element_type=F32)


def spread(row):
    return jnp.broadcast_to(row, (LANES, LANES)).T


def lse_pass(z_ref, b_ref, rows, cols, put):
    width, depth = 2, 128

    @pl.loop(0, cols // (width * LANES))
    def _(col):
        def block(n, state):
            at = pl.ds(pl.multiple_of(n * depth, depth), depth)
            out = []
            for k in range(width):
                top, total = state[k]
                lane = pl.multiple_of(col * width * LANES + k * LANES, LANES)
                v = (z_ref[at, pl.ds(lane, LANES)] + b_ref[at, :]).reshape(depth // 8, 8, LANES)
                new = jnp.maximum(top, jnp.max(v, axis=0))
                total = total * jnp.exp2(top - new) + jnp.sum(jnp.exp2(v - new[None]), axis=0)
                out.append((new, total))
            return tuple(out)

        start = (jnp.full((8, LANES), -jnp.inf, F32), jnp.zeros((8, LANES), F32))
        state = lax.fori_loop(0, rows // depth, block, (start,) * width, unroll=4)
        for k in range(width):
            top, total = state[k]
            best = jnp.max(top, axis=0, keepdims=True)
            total = jnp.sum(total * jnp.exp2(top - best), axis=0, keepdims=True)
            put(col * width + k, best + LOG2E * jnp.log(total))


def combine(parts):
    top = jnp.max(parts, axis=0)
    return top + LOG2E * jnp.log(jnp.sum(jnp.exp2(parts - top[None]), axis=0))


def kernel(
    x_ref, y_ref, la_ref, lb_ref, sp_ref, tp_ref, out_ref,
    xa, xt, ya, yt, zt, z, qb, pb, nx, ny,
    l_row, rs, pg, l_col, cr, qs, qg, tg, xs, xf, yf, mf, sf, acc, part, shares,
    rs_sem, pg_sem, cr_sem, qg_sem, tr_send, tr_recv, or_send, or_recv, xs_sem, part_sem,
):
    s, t = lax.axis_index("src"), lax.axis_index("tgt")
    gx, gy, core = s // (GRID_Y * 2), lax.rem(s // 2, GRID_Y), lax.rem(s, 2)
    me = gx * 2 + core

    def z_peer(k):
        return lax.rem(t + k, NTGT)

    def s_peer(k):
        return lax.rem(s + k, NSRC)

    def mate(e):
        return ((e // 2) * GRID_Y + gy) * 2 + lax.rem(e, 2)

    barrier = pltpu.get_barrier_semaphore()

    @pl.loop(1, NTGT)
    def _(k):
        pl.semaphore_signal(barrier, inc=1, device_id=(s, z_peer(k)), device_id_type=MESH)

    @pl.loop(1, NSRC)
    def _(k):
        pl.semaphore_signal(barrier, inc=1, device_id=(s_peer(k), t), device_id_type=MESH)

    def remote(src, dst, send, recv, device):
        return pltpu.make_async_remote_copy(
            src_ref=src, dst_ref=dst, send_sem=send, recv_sem=recv, device_id=device, device_id_type=MESH
        )

    def wait_bytes(ref, sem):
        remote(ref, ref, sem, sem, (s, t)).wait_recv()

    @pl.loop(0, RCH, unroll=2)
    def _(k):
        at = pl.ds(pl.multiple_of(k * LANES, LANES), LANES)
        x = x_ref[at, :]
        turned = x.T
        nx[k] = jnp.sum(turned * turned, axis=0, keepdims=True)
        xa[at, :] = split3(x * (2.0 * LOG2E), (0, 0, 1))
        xt[:, at] = split3(turned * (2.0 * LOG2E), (0, 0, 1), axis=0)

    for k in range(CCH):
        at = slice(k * LANES, (k + 1) * LANES)
        y = y_ref[at, :]
        turned = y.T
        ny[k : k + 1, :] = jnp.sum(turned * turned, axis=0, keepdims=True)
        ya[at, :] = split3(y, (0, 1, 0))
        yt[:, at] = split3(turned, (0, 1, 0), axis=0)
        qb[at, :] = spread(-LOG2E * ny[k : k + 1, :])

    tg[t] = y_ref[pl.ds(pl.multiple_of(me * PIECE, PIECE), PIECE), :]
    own_rows = pl.ds(pl.multiple_of(t * OWN, OWN), OWN)
    xs[me] = x_ref[own_rows, :]

    @pl.loop(0, ROWS // 256)
    def _(k):
        at = pl.ds(pl.multiple_of(k * 256, 256), 256)
        zt[:, at] = dot(ya[...], xt[:, at])

    pl.semaphore_wait(barrier, NTGT - 1 + NSRC - 1)

    def hops(way, chunk):
        return NTGT // 2 - (way ^ chunk)

    def ring_step(view, send, recv, step):
        for chunk in range(2):
            for way in range(2):
                if step > hops(way, chunk):
                    continue
                block = lax.rem(t + (NTGT - step if way == 0 else step), NTGT)
                ref = view(chunk, block)
                if step > 0:
                    wait_bytes(ref, recv.at[way, chunk, step - 1])
                if step < hops(way, chunk):
                    to = lax.rem(t + (1 if way == 0 else NTGT - 1), NTGT)
                    remote(ref, ref, send.at[way, chunk], recv.at[way, chunk, step], (s, to)).start()

    def t_view(chunk, block):
        return tg.at[block, pl.ds(chunk * (PIECE // 2), PIECE // 2), :]

    def t_step(step):
        ring_step(t_view, tr_send, tr_recv, step)

    t_step(0)

    @pl.loop(1, MATES)
    def _(k):
        to = mate(lax.rem(me + k, MATES))
        remote(xs.at[me], xs.at[me], xs_sem.at[0], xs_sem.at[1], (to, t)).start()

    for it in range(ITERS):

        def put_row(chunk, value):
            l_row[it, chunk] = value

        lse_pass(zt, qb, COLS, ROWS, put_row)
        rs[it, t] = l_row[it, t]

        @pl.loop(1, NTGT)
        def _(k):
            to = z_peer(k)
            remote(l_row.at[it, to], rs.at[it, t], rs_sem.at[it, 0], rs_sem.at[it, 1], (s, to)).start()

        if it == 0:
            t_step(1)
            for half in range(2):
                @pl.loop(half * 2, half * 2 + 2)
                def _(k):
                    at = pl.ds(pl.multiple_of(k * 256, 256), 256)
                    z[:, at] = dot(xa[...], yt[:, at])

                t_step(2 + half)
        else:
            t_step(7)

        wait_bytes(rs.at[it, pl.ds(0, NTGT - 1)], rs_sem.at[it, 1])
        pg[it, t] = LOG2E * la_ref[t] - combine(rs[it])

        @pl.loop(1, NTGT)
        def _(k):
            remote(pg.at[it, t], pg.at[it, t], pg_sem.at[it, 0], pg_sem.at[it, 1], (s, z_peer(k))).start()

        t_step(4 if it == 0 else 8)
        wait_bytes(pg.at[it, pl.ds(0, NTGT - 1)], pg_sem.at[it, 1])
        for k in range(RCH):
            pb[k * LANES : (k + 1) * LANES, :] = spread(pg[it, k])

        def put_col(chunk, value):
            l_col[it, pl.ds(chunk, 1), :] = value

        lse_pass(z, pb, ROWS, COLS, put_col)

        @pl.loop(1, NSRC)
        def _(k):
            remote(l_col.at[it], cr.at[it, s], cr_sem.at[it, 0], cr_sem.at[it, 1], (s_peer(k), t)).start()

        cr[it, s] = l_col[it]
        if it == 0:
            t_step(5)
        else:
            sp_ref[...] = pg[it] * LN2 + nx[...]
            wait_bytes(xs.at[pl.ds(0, MATES - 1)], xs_sem.at[1])

            @pl.loop(0, MATES)
            def _(e):
                at = pl.ds(pl.multiple_of(e * OWN, OWN), OWN)
                xf[at, :] = split3(xs[e] * (2.0 * LOG2E), (0, 0, 1))

            @pl.loop(0, NTGT // 2)
            def _(b):
                at = pl.ds(pl.multiple_of(b * 2 * PIECE, 2 * PIECE), 2 * PIECE)
                y = tg[pl.ds(b * 2, 2)].reshape(2 * PIECE, LATENT)
                yf[at, :] = split3(y, (0, 1))
                zt[:, at] = dot(xf[...], split3(y.T, (0, 1, 0), axis=0))

        wait_bytes(cr.at[it, pl.ds(0, NSRC - 1)], cr_sem.at[it, 1])
        q = LOG2E * lb_ref[...] - combine(cr[it])
        if it == 0:
            for k in range(CCH):
                qb[k * LANES : (k + 1) * LANES, :] = spread(q[k : k + 1, :])
            t_step(6)

    for k in range(CCH):
        qs[k] = q[k : k + 1, :]
    qg[t] = qs[me]

    @pl.loop(1, NTGT)
    def _(k):
        remote(qs.at[me], qg.at[t], qg_sem.at[0], qg_sem.at[1], (s, z_peer(k))).start()

    tp_ref[...] = q * LN2 + ny[...]
    wait_bytes(qg.at[pl.ds(0, NTGT - 1)], qg_sem.at[1])

    depth = 64
    for far in (2, 1, 3, 0):
        chip = lax.rem(gx + far, GRID_X)
        base = chip * 2 * OWN

        @pl.loop(0, 2 * OWN // depth)
        def _(r):
            at = pl.ds(pl.multiple_of(base + r * depth, depth), depth)
            best = zt[at, 0:LANES] + qg[0]
            for b in range(1, NTGT):
                best = jnp.maximum(best, zt[at, b * LANES : (b + 1) * LANES] + qg[b])
            to = pl.ds(pl.multiple_of(r * depth, depth), depth)
            mf[to, :] = jnp.broadcast_to(jnp.max(best, axis=1, keepdims=True), (depth, LANES))

        sf[...] = jnp.zeros_like(sf)
        acc[...] = jnp.zeros_like(acc)
        at = pl.ds(pl.multiple_of(base, 2 * OWN), 2 * OWN)
        group = 4

        @pl.loop(0, NTGT // group)
        def _(b):
            highs, lows = [], []
            total = sf[...]
            for k in range(group):
                lane = pl.ds(pl.multiple_of((b * group + k) * LANES, LANES), LANES)
                w = jnp.exp2(zt[at, lane] + qg[b * group + k] - mf[...])
                total += w
                high = w.astype(BF16)
                highs.append(high)
                lows.append((w - high.astype(F32)).astype(BF16))
            sf[...] = total
            ys = pl.ds(pl.multiple_of(b * group * LANES, group * LANES), group * LANES)
            both = jnp.dot(jnp.concatenate(highs, axis=1), yf[ys, 0 : 2 * LATENT], preferred_element_type=F32)
            rest = jnp.dot(jnp.concatenate(lows, axis=1), yf[ys, 0:LATENT], preferred_element_type=F32)
            acc[...] += both[:, :LATENT] + both[:, LATENT:] + rest

        for g in range(2):
            rows = slice(g * OWN, (g + 1) * OWN)
            to = chip * 2 + g
            part[to, 0:OWN, :] = acc[rows, :]
            part[to, OWN : OWN + 1, :] = mf[rows, :].T[0:1, :]
            part[to, OWN + 1 : OWN + 2, :] = jnp.sum(sf[rows, :].T, axis=0, keepdims=True)

            def send():
                remote(part.at[to], shares.at[me], part_sem.at[0], part_sem.at[1], (mate(to), t)).start()

            if far == 0:
                pl.when(core != g)(send)
            else:
                send()

    shares[me, 0 : OWN + 2, :] = part[me, 0 : OWN + 2, :]
    wait_bytes(shares.at[pl.ds(0, MATES - 1)], part_sem.at[1])
    tops = [shares[e, OWN : OWN + 1, :] for e in range(MATES)]
    best = tops[0]
    for v in tops[1:]:
        best = jnp.maximum(best, v)
    scales = [jnp.exp2(v - best) for v in tops]
    total = sum(scales[e] * shares[e, OWN + 1 : OWN + 2, :] for e in range(MATES))
    out = jnp.zeros((OWN, LATENT), F32)
    for e in range(MATES):
        out += spread(scales[e] / total) * shares[e, 0:OWN, :]
    out_ref[own_rows, :] = out

    def o_view(chunk, block):
        rows = OWN // 2
        return out_ref.at[pl.ds(pl.multiple_of(block * OWN + chunk * rows, rows), rows), :]

    for step in range(NTGT // 2 + 1):
        ring_step(o_view, or_send, or_recv, step)

    for chunk in range(2):
        for way in range(2):
            n = hops(way, chunk)
            wait_bytes(tg.at[pl.ds(0, n), pl.ds(0, PIECE // 2), :], tr_send.at[way, chunk])
            wait_bytes(out_ref.at[pl.ds(0, n * (OWN // 2)), :], or_send.at[way, chunk])
    wait_bytes(xs.at[pl.ds(0, MATES - 1)], xs_sem.at[0])
    wait_bytes(part.at[pl.ds(0, MATES - 1)], part_sem.at[0])
    for it in range(ITERS):
        wait_bytes(rs.at[it, pl.ds(0, NTGT - 1)], rs_sem.at[it, 0])
        wait_bytes(pg.at[it, pl.ds(0, NTGT - 1)], pg_sem.at[it, 0])
        wait_bytes(cr.at[it, pl.ds(0, NSRC - 1)], cr_sem.at[it, 0])
    wait_bytes(qg.at[pl.ds(0, NTGT - 1)], qg_sem.at[0])


def on_device(sources, targets, log_source, log_target):
    vmem = pl.BlockSpec(memory_space=pltpu.VMEM)
    dma = pltpu.SemaphoreType.DMA
    sp, tp, bary = pl.pallas_call(
        kernel,
        out_shape=(
            jax.ShapeDtypeStruct((RCH, 1, LANES), F32),
            jax.ShapeDtypeStruct((CCH, LANES), F32),
            jax.ShapeDtypeStruct((ROWS, LATENT), F32),
        ),
        in_specs=[vmem] * 4,
        out_specs=(vmem,) * 3,
        scratch_shapes=[
            pltpu.VMEM((ROWS, 3 * LATENT), BF16),
            pltpu.VMEM((3 * LATENT, ROWS), BF16),
            pltpu.VMEM((COLS, 3 * LATENT), BF16),
            pltpu.VMEM((3 * LATENT, COLS), BF16),
            pltpu.VMEM((COLS, ROWS), F32),
            pltpu.VMEM((ROWS, COLS), F32),
            pltpu.VMEM((COLS, LANES), F32),
            pltpu.VMEM((ROWS, LANES), F32),
            pltpu.VMEM((RCH, 1, LANES), F32),
            pltpu.VMEM((CCH, LANES), F32),
            pltpu.VMEM((ITERS, RCH, 1, LANES), F32),
            pltpu.VMEM((ITERS, NTGT, 1, LANES), F32),
            pltpu.VMEM((ITERS, RCH, 1, LANES), F32),
            pltpu.VMEM((ITERS, CCH, LANES), F32),
            pltpu.VMEM((ITERS, NSRC, CCH, LANES), F32),
            pltpu.VMEM((CCH, 1, LANES), F32),
            pltpu.VMEM((NTGT, 1, LANES), F32),
            pltpu.VMEM((NTGT, PIECE, LATENT), F32),
            pltpu.VMEM((MATES, OWN, LATENT), F32),
            pltpu.VMEM((MATES * OWN, 3 * LATENT), BF16),
            pltpu.VMEM((NTGT * PIECE, 2 * LATENT), BF16),
            pltpu.VMEM((2 * OWN, LANES), F32),
            pltpu.VMEM((2 * OWN, LANES), F32),
            pltpu.VMEM((2 * OWN, LATENT), F32),
            pltpu.VMEM((MATES, OWN + 8, LATENT), F32),
            pltpu.VMEM((MATES, OWN + 8, LATENT), F32),
            dma((ITERS, 2)),
            dma((ITERS, 2)),
            dma((ITERS, 2)),
            dma((2,)),
            dma((2, 2)), dma((2, 2, 8)),
            dma((2, 2)), dma((2, 2, 8)),
            dma((2,)),
            dma((2,)),
        ],
        compiler_params=pltpu.CompilerParams(
            collective_id=0, has_side_effects=True, vmem_limit_bytes=56 * 2**20
        ),
        cost_estimate=pl.CostEstimate(flops=6 * 10**9, bytes_accessed=4 * 2**20, transcendentals=10**7),
        name="coupling",
    )(
        sources,
        targets,
        log_source.reshape(RCH, 1, LANES),
        log_target.reshape(CCH, LANES),
    )
    return sp.reshape(ROWS), tp.reshape(COLS), bary


def solution(mesh):
    in_specs = (P("src", None), P("tgt", None), P("src"), P("tgt"))
    out_specs = (P("src"), P("tgt"), P("src", None))
    return jax.shard_map(
        on_device, mesh=mesh, in_specs=in_specs, out_specs=out_specs, check_vma=False
    )
```

```python
import math

import jax
import jax.numpy as jnp
from jax import lax
from jax.experimental import pallas as pl
from jax.experimental.pallas import tpu as pltpu
from jax.sharding import PartitionSpec as P

ITERS = 2
LATENT = 128
LANES = 128
LOG2E = math.log2(math.e)
LN2 = math.log(2.0)
MESH = pl.DeviceIdType.MESH

NSRC, NTGT = 32, 16
GRID_X, GRID_Y = 4, 4
ROWS, COLS = 2048, 1024
RCH, CCH = ROWS // LANES, COLS // LANES
OWN = ROWS // NTGT
MATES = GRID_X * 2
PIECE = COLS // MATES
F32, BF16 = jnp.float32, jnp.bfloat16


def split3(v, order, axis=1):
    high = v.astype(BF16)
    low = (v - high.astype(F32)).astype(BF16)
    return jnp.concatenate([(high, low)[k] for k in order], axis=axis)


def dot(a, b):
    return jnp.dot(a, b, preferred_element_type=F32)


def spread(row):
    return jnp.broadcast_to(row, (LANES, LANES)).T


def lse_pass(z_ref, b_ref, rows, cols, put):
    width, depth = 2, 128

    @pl.loop(0, cols // (width * LANES))
    def _(col):
        def block(n, state):
            at = pl.ds(pl.multiple_of(n * depth, depth), depth)
            out = []
            for k in range(width):
                top, total = state[k]
                lane = pl.multiple_of(col * width * LANES + k * LANES, LANES)
                v = (z_ref[at, pl.ds(lane, LANES)] + b_ref[at, :]).reshape(depth // 8, 8, LANES)
                new = jnp.maximum(top, jnp.max(v, axis=0))
                total = total * jnp.exp2(top - new) + jnp.sum(jnp.exp2(v - new[None]), axis=0)
                out.append((new, total))
            return tuple(out)

        start = (jnp.full((8, LANES), -jnp.inf, F32), jnp.zeros((8, LANES), F32))
        state = lax.fori_loop(0, rows // depth, block, (start,) * width, unroll=4)
        for k in range(width):
            top, total = state[k]
            best = jnp.max(top, axis=0, keepdims=True)
            total = jnp.sum(total * jnp.exp2(top - best), axis=0, keepdims=True)
            put(col * width + k, best + LOG2E * jnp.log(total))


def combine(parts):
    top = jnp.max(parts, axis=0)
    return top + LOG2E * jnp.log(jnp.sum(jnp.exp2(parts - top[None]), axis=0))


def kernel(
    x_ref, y_ref, la_ref, lb_ref, sp_ref, tp_ref, out_ref,
    xa, xt, ya, yt, zt, z, qb, pb, nx, ny,
    l_row, rs, l_col, cr, qs, qg, tg, xs, xf, yf, mf, sf, acc, part, shares,
    rs_sem, cr_sem, qg_sem, tr_send, tr_recv, or_send, or_recv, xs_sem, part_sem,
):
    s, t = lax.axis_index("src"), lax.axis_index("tgt")
    gx, gy, core = s // (GRID_Y * 2), lax.rem(s // 2, GRID_Y), lax.rem(s, 2)
    me = gx * 2 + core

    def z_peer(k):
        return lax.rem(t + k, NTGT)

    def s_peer(k):
        return lax.rem(s + k, NSRC)

    def mate(e):
        return ((e // 2) * GRID_Y + gy) * 2 + lax.rem(e, 2)

    barrier = pltpu.get_barrier_semaphore()

    @pl.loop(1, NTGT)
    def _(k):
        pl.semaphore_signal(barrier, inc=1, device_id=(s, z_peer(k)), device_id_type=MESH)

    @pl.loop(1, NSRC)
    def _(k):
        pl.semaphore_signal(barrier, inc=1, device_id=(s_peer(k), t), device_id_type=MESH)

    def remote(src, dst, send, recv, device):
        return pltpu.make_async_remote_copy(
            src_ref=src, dst_ref=dst, send_sem=send, recv_sem=recv, device_id=device, device_id_type=MESH
        )

    def wait_bytes(ref, sem):
        remote(ref, ref, sem, sem, (s, t)).wait_recv()

    @pl.loop(0, RCH, unroll=2)
    def _(k):
        at = pl.ds(pl.multiple_of(k * LANES, LANES), LANES)
        x = x_ref[at, :]
        turned = x.T
        nx[pl.ds(k, 1), :] = jnp.sum(turned * turned, axis=0, keepdims=True)
        xa[at, :] = split3(x * (2.0 * LOG2E), (0, 0, 1))
        xt[:, at] = split3(turned * (2.0 * LOG2E), (0, 0, 1), axis=0)

    for k in range(CCH):
        at = slice(k * LANES, (k + 1) * LANES)
        y = y_ref[at, :]
        turned = y.T
        ny[k : k + 1, :] = jnp.sum(turned * turned, axis=0, keepdims=True)
        ya[at, :] = split3(y, (0, 1, 0))
        yt[:, at] = split3(turned, (0, 1, 0), axis=0)
        qb[at, :] = spread(-LOG2E * ny[k : k + 1, :])

    tg[t] = y_ref[pl.ds(pl.multiple_of(me * PIECE, PIECE), PIECE), :]
    own_rows = pl.ds(pl.multiple_of(t * OWN, OWN), OWN)
    xs[me] = x_ref[own_rows, :]

    @pl.loop(0, ROWS // 256)
    def _(k):
        at = pl.ds(pl.multiple_of(k * 256, 256), 256)
        zt[:, at] = dot(ya[...], xt[:, at])

    pl.semaphore_wait(barrier, NTGT - 1 + NSRC - 1)

    def hops(way, chunk):
        return NTGT // 2 - (way ^ chunk)

    def ring_step(view, send, recv, step):
        for chunk in range(2):
            for way in range(2):
                if step > hops(way, chunk):
                    continue
                block = lax.rem(t + (NTGT - step if way == 0 else step), NTGT)
                ref = view(chunk, block)
                if step > 0:
                    wait_bytes(ref, recv.at[way, chunk, step - 1])
                if step < hops(way, chunk):
                    to = lax.rem(t + (1 if way == 0 else NTGT - 1), NTGT)
                    remote(ref, ref, send.at[way, chunk], recv.at[way, chunk, step], (s, to)).start()

    def t_view(chunk, block):
        return tg.at[block, pl.ds(chunk * (PIECE // 2), PIECE // 2), :]

    def t_step(step):
        ring_step(t_view, tr_send, tr_recv, step)

    t_step(0)

    @pl.loop(1, MATES)
    def _(k):
        to = mate(lax.rem(me + k, MATES))
        remote(xs.at[me], xs.at[me], xs_sem.at[0], xs_sem.at[1], (to, t)).start()

    for it in range(ITERS):

        def put_row(chunk, value):
            l_row[it, pl.ds(chunk, 1), :] = value

        lse_pass(zt, qb, COLS, ROWS, put_row)

        @pl.loop(1, NTGT)
        def _(k):
            remote(l_row.at[it], rs.at[it, t], rs_sem.at[it, 0], rs_sem.at[it, 1], (s, z_peer(k))).start()

        rs[it, t] = l_row[it]
        if it == 0:
            t_step(1)
            for half in range(2):
                @pl.loop(half * 2, half * 2 + 2)
                def _(k):
                    at = pl.ds(pl.multiple_of(k * 256, 256), 256)
                    z[:, at] = dot(xa[...], yt[:, at])

                t_step(2 + half)
        else:
            t_step(7)

        wait_bytes(rs.at[it, pl.ds(0, NTGT - 1)], rs_sem.at[it, 1])
        row_pot = LOG2E * la_ref[...] - combine(rs[it])
        for k in range(RCH):
            pb[k * LANES : (k + 1) * LANES, :] = spread(row_pot[k : k + 1, :])
        t_step(4 if it == 0 else 8)

        def put_col(chunk, value):
            l_col[it, pl.ds(chunk, 1), :] = value

        lse_pass(z, pb, ROWS, COLS, put_col)

        @pl.loop(1, NSRC)
        def _(k):
            remote(l_col.at[it], cr.at[it, s], cr_sem.at[it, 0], cr_sem.at[it, 1], (s_peer(k), t)).start()

        cr[it, s] = l_col[it]
        if it == 0:
            t_step(5)
        else:
            sp_ref[...] = row_pot * LN2 + nx[...]
            wait_bytes(xs.at[pl.ds(0, MATES - 1)], xs_sem.at[1])

            @pl.loop(0, MATES)
            def _(e):
                at = pl.ds(pl.multiple_of(e * OWN, OWN), OWN)
                xf[at, :] = split3(xs[e] * (2.0 * LOG2E), (0, 0, 1))

            @pl.loop(0, NTGT // 2)
            def _(b):
                at = pl.ds(pl.multiple_of(b * 2 * PIECE, 2 * PIECE), 2 * PIECE)
                y = tg[pl.ds(b * 2, 2)].reshape(2 * PIECE, LATENT)
                yf[at, :] = split3(y, (0, 1))
                zt[:, at] = dot(xf[...], split3(y.T, (0, 1, 0), axis=0))

        wait_bytes(cr.at[it, pl.ds(0, NSRC - 1)], cr_sem.at[it, 1])
        q = LOG2E * lb_ref[...] - combine(cr[it])
        if it == 0:
            for k in range(CCH):
                qb[k * LANES : (k + 1) * LANES, :] = spread(q[k : k + 1, :])
            t_step(6)

    for k in range(CCH):
        qs[k] = q[k : k + 1, :]
    qg[t] = qs[me]

    @pl.loop(1, NTGT)
    def _(k):
        remote(qs.at[me], qg.at[t], qg_sem.at[0], qg_sem.at[1], (s, z_peer(k))).start()

    tp_ref[...] = q * LN2 + ny[...]
    wait_bytes(qg.at[pl.ds(0, NTGT - 1)], qg_sem.at[1])

    depth = 64
    for far in (2, 1, 3, 0):
        chip = lax.rem(gx + far, GRID_X)
        base = chip * 2 * OWN

        @pl.loop(0, 2 * OWN // depth)
        def _(r):
            at = pl.ds(pl.multiple_of(base + r * depth, depth), depth)
            best = zt[at, 0:LANES] + qg[0]
            for b in range(1, NTGT):
                best = jnp.maximum(best, zt[at, b * LANES : (b + 1) * LANES] + qg[b])
            to = pl.ds(pl.multiple_of(r * depth, depth), depth)
            mf[to, :] = jnp.broadcast_to(jnp.max(best, axis=1, keepdims=True), (depth, LANES))

        sf[...] = jnp.zeros_like(sf)
        acc[...] = jnp.zeros_like(acc)
        at = pl.ds(pl.multiple_of(base, 2 * OWN), 2 * OWN)
        group = 4

        @pl.loop(0, NTGT // group)
        def _(b):
            highs, lows = [], []
            total = sf[...]
            for k in range(group):
                lane = pl.ds(pl.multiple_of((b * group + k) * LANES, LANES), LANES)
                w = jnp.exp2(zt[at, lane] + qg[b * group + k] - mf[...])
                total += w
                high = w.astype(BF16)
                highs.append(high)
                lows.append((w - high.astype(F32)).astype(BF16))
            sf[...] = total
            ys = pl.ds(pl.multiple_of(b * group * LANES, group * LANES), group * LANES)
            both = jnp.dot(jnp.concatenate(highs, axis=1), yf[ys, 0 : 2 * LATENT], preferred_element_type=F32)
            rest = jnp.dot(jnp.concatenate(lows, axis=1), yf[ys, 0:LATENT], preferred_element_type=F32)
            acc[...] += both[:, :LATENT] + both[:, LATENT:] + rest

        for g in range(2):
            rows = slice(g * OWN, (g + 1) * OWN)
            to = chip * 2 + g
            part[to, 0:OWN, :] = acc[rows, :]
            part[to, OWN : OWN + 1, :] = mf[rows, :].T[0:1, :]
            part[to, OWN + 1 : OWN + 2, :] = jnp.sum(sf[rows, :].T, axis=0, keepdims=True)

            def send():
                remote(part.at[to], shares.at[me], part_sem.at[0], part_sem.at[1], (mate(to), t)).start()

            if far == 0:
                pl.when(core != g)(send)
            else:
                send()

    shares[me, 0 : OWN + 2, :] = part[me, 0 : OWN + 2, :]
    wait_bytes(shares.at[pl.ds(0, MATES - 1)], part_sem.at[1])
    tops = [shares[e, OWN : OWN + 1, :] for e in range(MATES)]
    best = tops[0]
    for v in tops[1:]:
        best = jnp.maximum(best, v)
    scales = [jnp.exp2(v - best) for v in tops]
    total = sum(scales[e] * shares[e, OWN + 1 : OWN + 2, :] for e in range(MATES))
    out = jnp.zeros((OWN, LATENT), F32)
    for e in range(MATES):
        out += spread(scales[e] / total) * shares[e, 0:OWN, :]
    out_ref[own_rows, :] = out

    def o_view(chunk, block):
        rows = OWN // 2
        return out_ref.at[pl.ds(pl.multiple_of(block * OWN + chunk * rows, rows), rows), :]

    for step in range(NTGT // 2 + 1):
        ring_step(o_view, or_send, or_recv, step)

    for chunk in range(2):
        for way in range(2):
            n = hops(way, chunk)
            wait_bytes(tg.at[pl.ds(0, n), pl.ds(0, PIECE // 2), :], tr_send.at[way, chunk])
            wait_bytes(out_ref.at[pl.ds(0, n * (OWN // 2)), :], or_send.at[way, chunk])
    wait_bytes(xs.at[pl.ds(0, MATES - 1)], xs_sem.at[0])
    wait_bytes(part.at[pl.ds(0, MATES - 1)], part_sem.at[0])
    for it in range(ITERS):
        wait_bytes(rs.at[it, pl.ds(0, NTGT - 1)], rs_sem.at[it, 0])
        wait_bytes(cr.at[it, pl.ds(0, NSRC - 1)], cr_sem.at[it, 0])
    wait_bytes(qg.at[pl.ds(0, NTGT - 1)], qg_sem.at[0])


def on_device(sources, targets, log_source, log_target):
    vmem = pl.BlockSpec(memory_space=pltpu.VMEM)
    dma = pltpu.SemaphoreType.DMA
    sp, tp, bary = pl.pallas_call(
        kernel,
        out_shape=(
            jax.ShapeDtypeStruct((RCH, LANES), F32),
            jax.ShapeDtypeStruct((CCH, LANES), F32),
            jax.ShapeDtypeStruct((ROWS, LATENT), F32),
        ),
        in_specs=[vmem] * 4,
        out_specs=(vmem,) * 3,
        scratch_shapes=[
            pltpu.VMEM((ROWS, 3 * LATENT), BF16),
            pltpu.VMEM((3 * LATENT, ROWS), BF16),
            pltpu.VMEM((COLS, 3 * LATENT), BF16),
            pltpu.VMEM((3 * LATENT, COLS), BF16),
            pltpu.VMEM((COLS, ROWS), F32),
            pltpu.VMEM((ROWS, COLS), F32),
            pltpu.VMEM((COLS, LANES), F32),
            pltpu.VMEM((ROWS, LANES), F32),
            pltpu.VMEM((RCH, LANES), F32),
            pltpu.VMEM((CCH, LANES), F32),
            pltpu.VMEM((ITERS, RCH, LANES), F32),
            pltpu.VMEM((ITERS, NTGT, RCH, LANES), F32),
            pltpu.VMEM((ITERS, CCH, LANES), F32),
            pltpu.VMEM((ITERS, NSRC, CCH, LANES), F32),
            pltpu.VMEM((CCH, 1, LANES), F32),
            pltpu.VMEM((NTGT, 1, LANES), F32),
            pltpu.VMEM((NTGT, PIECE, LATENT), F32),
            pltpu.VMEM((MATES, OWN, LATENT), F32),
            pltpu.VMEM((MATES * OWN, 3 * LATENT), BF16),
            pltpu.VMEM((NTGT * PIECE, 2 * LATENT), BF16),
            pltpu.VMEM((2 * OWN, LANES), F32),
            pltpu.VMEM((2 * OWN, LANES), F32),
            pltpu.VMEM((2 * OWN, LATENT), F32),
            pltpu.VMEM((MATES, OWN + 8, LATENT), F32),
            pltpu.VMEM((MATES, OWN + 8, LATENT), F32),
            dma((ITERS, 2)),
            dma((ITERS, 2)),
            dma((2,)),
            dma((2, 2)), dma((2, 2, 8)),
            dma((2, 2)), dma((2, 2, 8)),
            dma((2,)),
            dma((2,)),
        ],
        compiler_params=pltpu.CompilerParams(
            collective_id=0, has_side_effects=True, vmem_limit_bytes=56 * 2**20
        ),
        cost_estimate=pl.CostEstimate(flops=6 * 10**9, bytes_accessed=4 * 2**20, transcendentals=10**7),
        name="coupling",
    )(
        sources,
        targets,
        log_source.reshape(RCH, LANES),
        log_target.reshape(CCH, LANES),
    )
    return sp.reshape(ROWS), tp.reshape(COLS), bary


def solution(mesh):
    in_specs = (P("src", None), P("tgt", None), P("src"), P("tgt"))
    out_specs = (P("src"), P("tgt"), P("src", None))
    return jax.shard_map(
        on_device, mesh=mesh, in_specs=in_specs, out_specs=out_specs, check_vma=False
    )
```

```python
import functools
import math

import jax
import jax.numpy as jnp
from jax import lax
from jax.experimental import pallas as pl
from jax.experimental.pallas import tpu as pltpu
from jax.sharding import PartitionSpec as P

ITERS = 2
LATENT = 128
LANES = 128
LOG2E = math.log2(math.e)
LN2 = math.log(2.0)
MESH = pl.DeviceIdType.MESH

NSRC, NTGT = 32, 16
GRID_X, GRID_Y = 4, 4
ROWS, COLS = 2048, 1024
RCH, CCH = ROWS // LANES, COLS // LANES
OWN = ROWS // NTGT
O_CHUNKS = 4
MATES = GRID_X * 2
DELIVERIES = 8
PIECE = COLS // MATES
F32, BF16 = jnp.float32, jnp.bfloat16


def split3(v, order, axis=1):
    high = v.astype(BF16)
    low = (v - high.astype(F32)).astype(BF16)
    return jnp.concatenate([(high, low)[k] for k in order], axis=axis)


def dot(a, b):
    return jnp.dot(a, b, preferred_element_type=F32)


def spread(row):
    return jnp.broadcast_to(row, (LANES, LANES)).T


def lse_down(z_ref, b_ref, top_ref, total_ref):
    rows, cols = z_ref.shape
    width, depth = 2, 128

    @pl.loop(0, cols // (width * LANES))
    def _(col):
        def block(n, state):
            at = pl.ds(pl.multiple_of(n * depth, depth), depth)
            out = []
            for k in range(width):
                top, total = state[k]
                lane = pl.multiple_of(col * width * LANES + k * LANES, LANES)
                v = (z_ref[at, pl.ds(lane, LANES)] + b_ref[at, :]).reshape(depth // 8, 8, LANES)
                new = jnp.maximum(top, jnp.max(v, axis=0))
                total = total * jnp.exp2(top - new) + jnp.sum(jnp.exp2(v - new[None]), axis=0)
                out.append((new, total))
            return tuple(out)

        start = (jnp.full((8, LANES), -jnp.inf, F32), jnp.zeros((8, LANES), F32))
        state = lax.fori_loop(0, rows // depth, block, (start,) * width, unroll=True)
        for k in range(width):
            top_ref[col * width + k], total_ref[col * width + k] = state[k]

    tops = top_ref[...]
    best = jnp.max(tops, axis=1)
    total = jnp.sum(total_ref[...] * jnp.exp2(tops - best[:, None, :]), axis=1)
    return best + LOG2E * jnp.log(total)


def lse_across(z_ref, b_ref, top_ref, total_ref, out_ref):
    rows, cols = z_ref.shape
    depth = 16

    @pl.loop(0, rows // depth, unroll=4)
    def _(n):
        at = pl.ds(pl.multiple_of(n * depth, depth), depth)
        v = [z_ref[at, c * LANES : (c + 1) * LANES] + b_ref[c : c + 1, :] for c in range(cols // LANES)]
        top = functools.reduce(jnp.maximum, v)
        top_ref[at, :] = top
        total_ref[at, :] = sum(jnp.exp2(x - top) for x in v)

    for k in range(rows // LANES):
        at = slice(k * LANES, (k + 1) * LANES)
        top = top_ref[at, :].T
        best = jnp.max(top, axis=0, keepdims=True)
        total = jnp.sum(total_ref[at, :].T * jnp.exp2(top - best), axis=0, keepdims=True)
        out_ref[k : k + 1, :] = best + LOG2E * jnp.log(total)


def combine(parts):
    top = jnp.max(parts, axis=0)
    return top + LOG2E * jnp.log(jnp.sum(jnp.exp2(parts - top[None]), axis=0))


def kernel(
    x_ref, y_ref, la_ref, lb_ref, sp_ref, tp_ref, out_ref,
    xt, ya, zt, zf, qb, pv, nx, ny, top8, total8, tops, totals,
    l_row, rs, l_col, cr, qs, qg, tg, xs, xf, yf, mf, sf, acc, part, shares,
    rs_sem, cr_sem, qg_sem, tr_send, tr_recv, or_send, or_recv, xs_sem, part_sem,
):
    s, t = lax.axis_index("src"), lax.axis_index("tgt")
    gx, gy, core = s // (GRID_Y * 2), lax.rem(s // 2, GRID_Y), lax.rem(s, 2)
    me = gx * 2 + core

    def z_peer(k):
        return lax.rem(t + k, NTGT)

    def s_peer(k):
        return lax.rem(s + k, NSRC)

    def mate(e):
        return ((e // 2) * GRID_Y + gy) * 2 + lax.rem(e, 2)

    barrier = pltpu.get_barrier_semaphore()

    @pl.loop(1, NTGT)
    def _(k):
        pl.semaphore_signal(barrier, inc=1, device_id=(s, z_peer(k)), device_id_type=MESH)

    @pl.loop(1, NSRC)
    def _(k):
        pl.semaphore_signal(barrier, inc=1, device_id=(s_peer(k), t), device_id_type=MESH)

    def remote(src, dst, send, recv, device):
        return pltpu.make_async_remote_copy(
            src_ref=src, dst_ref=dst, send_sem=send, recv_sem=recv, device_id=device, device_id_type=MESH
        )

    def wait_bytes(ref, sem):
        remote(ref, ref, sem, sem, (s, t)).wait_recv()

    @pl.loop(0, RCH, unroll=4)
    def _(k):
        at = pl.ds(pl.multiple_of(k * LANES, LANES), LANES)
        xt[:, at] = split3(x_ref[at, :].T * (2.0 * LOG2E), (0, 0, 1), axis=0)

    @pl.loop(0, CCH, unroll=2)
    def _(k):
        at = pl.ds(pl.multiple_of(k * LANES, LANES), LANES)
        y = y_ref[at, :]
        ya[at, :] = split3(y, (0, 1, 0))
        qb[at, :] = jnp.broadcast_to(-LOG2E * jnp.sum(y * y, axis=1, keepdims=True), (LANES, LANES))

    tg[t] = y_ref[pl.ds(pl.multiple_of(me * PIECE, PIECE), PIECE), :]
    own_rows = pl.ds(pl.multiple_of(t * OWN, OWN), OWN)
    xs[me] = x_ref[own_rows, :]

    @pl.loop(0, ROWS // 256)
    def _(k):
        at = pl.ds(pl.multiple_of(k * 256, 256), 256)
        zt[:, at] = dot(ya[...], xt[:, at])

    pl.semaphore_wait(barrier, NTGT - 1 + NSRC - 1)

    def hops(way, chunk):
        return NTGT // 2 - (way ^ chunk % 2)

    def ring_step(view, send, recv, step, chunks=2):
        for chunk in range(chunks):
            for way in range(2):
                if step > hops(way, chunk):
                    continue
                block = lax.rem(t + (NTGT - step if way == 0 else step), NTGT)
                ref = view(chunk, block)
                if step > 0:
                    wait_bytes(ref, recv.at[way, chunk, step - 1])
                if step < hops(way, chunk):
                    to = lax.rem(t + (1 if way == 0 else NTGT - 1), NTGT)
                    remote(ref, ref, send.at[way, chunk], recv.at[way, chunk, step], (s, to)).start()

    def t_view(chunk, block):
        return tg.at[block, pl.ds(chunk * (PIECE // 2), PIECE // 2), :]

    def t_step(step):
        ring_step(t_view, tr_send, tr_recv, step)

    t_step(0)

    @pl.loop(1, MATES)
    def _(k):
        to = mate(lax.rem(me + k, MATES))
        remote(xs.at[me], xs.at[me], xs_sem.at[0], xs_sem.at[1], (to, t)).start()

    def last_scores(first, last):
        @pl.loop(first, last)
        def _(b):
            at = pl.ds(pl.multiple_of(b * 2 * PIECE, 2 * PIECE), 2 * PIECE)
            y = tg[pl.ds(b * 2, 2)].reshape(2 * PIECE, LATENT)
            yf[at, :] = split3(y, (0, 1))
            zf[:, at] = dot(xf[...], split3(y.T, (0, 1, 0), axis=0))

    def last_rows(first, last):
        @pl.loop(first, last)
        def _(e):
            at = pl.ds(pl.multiple_of(e * OWN, OWN), OWN)
            xf[at, :] = split3(xs[e] * (2.0 * LOG2E), (0, 0, 1))

    for it in range(ITERS):
        l_row[it] = lse_down(zt, qb, top8, total8)

        @pl.loop(1, NTGT)
        def _(k):
            remote(l_row.at[it], rs.at[it, t], rs_sem.at[it, 0], rs_sem.at[it, 1], (s, z_peer(k))).start()

        rs[it, t] = l_row[it]
        if it == 0:
            t_step(1)
            for k in range(RCH):
                turned = x_ref[k * LANES : (k + 1) * LANES, :].T
                nx[k : k + 1, :] = jnp.sum(turned * turned, axis=0, keepdims=True)
            for k in range(CCH):
                turned = y_ref[k * LANES : (k + 1) * LANES, :].T
                ny[k : k + 1, :] = jnp.sum(turned * turned, axis=0, keepdims=True)
            t_step(2)
        else:
            t_step(8)
            last_scores(0, NTGT // 4)

        wait_bytes(rs.at[it, pl.ds(0, NTGT - 1)], rs_sem.at[it, 1])
        row_pot = LOG2E * la_ref[...] - combine(rs[it])
        pv[...] = row_pot
        if it == 0:
            t_step(3)
        lse_across(zt, pv, tops, totals, l_col.at[it])

        @pl.loop(1, NSRC)
        def _(k):
            remote(l_col.at[it], cr.at[it, s], cr_sem.at[it, 0], cr_sem.at[it, 1], (s_peer(k), t)).start()

        cr[it, s] = l_col[it]
        if it == 0:
            t_step(4)
            wait_bytes(xs.at[pl.ds(0, MATES - 1)], xs_sem.at[1])
            last_rows(0, MATES // 2)
            t_step(5)
            last_rows(MATES // 2, MATES)
            t_step(6)
        else:
            sp_ref[...] = row_pot * LN2 + nx[...]
            last_scores(NTGT // 4, NTGT // 2)

        wait_bytes(cr.at[it, pl.ds(0, NSRC - 1)], cr_sem.at[it, 1])
        q = LOG2E * lb_ref[...] - combine(cr[it])
        if it == 0:
            for k in range(CCH):
                qb[k * LANES : (k + 1) * LANES, :] = spread(q[k : k + 1, :])
            t_step(7)

    for k in range(CCH):
        qs[k] = q[k : k + 1, :]
    qg[t] = qs[me]

    @pl.loop(1, NTGT)
    def _(k):
        remote(qs.at[me], qg.at[t], qg_sem.at[0], qg_sem.at[1], (s, z_peer(k))).start()

    tp_ref[...] = q * LN2 + ny[...]
    wait_bytes(qg.at[pl.ds(0, NTGT - 1)], qg_sem.at[1])

    depth = 64
    for far in (2, 1, 3, 0):
        chip = lax.rem(gx + far, GRID_X)
        base = chip * 2 * OWN

        @pl.loop(0, 2 * OWN // depth)
        def _(r):
            at = pl.ds(pl.multiple_of(base + r * depth, depth), depth)
            best = zf[at, 0:LANES] + qg[0]
            for b in range(1, NTGT):
                best = jnp.maximum(best, zf[at, b * LANES : (b + 1) * LANES] + qg[b])
            to = pl.ds(pl.multiple_of(r * depth, depth), depth)
            mf[to, :] = jnp.broadcast_to(jnp.max(best, axis=1, keepdims=True), (depth, LANES))

        sf[...] = jnp.zeros_like(sf)
        acc[...] = jnp.zeros_like(acc)
        at = pl.ds(pl.multiple_of(base, 2 * OWN), 2 * OWN)
        group = 4

        @pl.loop(0, NTGT // group, unroll=2)
        def _(b):
            highs, lows = [], []
            total = sf[...]
            for k in range(group):
                lane = pl.ds(pl.multiple_of((b * group + k) * LANES, LANES), LANES)
                w = jnp.exp2(zf[at, lane] + qg[b * group + k] - mf[...])
                total += w
                high = w.astype(BF16)
                highs.append(high)
                lows.append((w - high.astype(F32)).astype(BF16))
            sf[...] = total
            ys = pl.ds(pl.multiple_of(b * group * LANES, group * LANES), group * LANES)
            both = jnp.dot(jnp.concatenate(highs, axis=1), yf[ys, 0 : 2 * LATENT], preferred_element_type=F32)
            rest = jnp.dot(jnp.concatenate(lows, axis=1), yf[ys, 0:LATENT], preferred_element_type=F32)
            acc[...] += both[:, :LATENT] + both[:, LATENT:] + rest

        for g in range(2):
            rows = slice(g * OWN, (g + 1) * OWN)
            to = chip * 2 + g
            part[to, 0:OWN, :] = acc[rows, :]
            part[to, OWN : OWN + 1, :] = mf[rows, :].T[0:1, :]
            part[to, OWN + 1 : OWN + 2, :] = jnp.sum(sf[rows, :].T, axis=0, keepdims=True)

            def send():
                remote(part.at[to], shares.at[me], part_sem.at[0], part_sem.at[1], (mate(to), t)).start()

            if far == 0:
                pl.when(core != g)(send)
            else:
                send()

    shares[me, 0 : OWN + 2, :] = part[me, 0 : OWN + 2, :]
    wait_bytes(shares.at[pl.ds(0, MATES - 1)], part_sem.at[1])
    tops = [shares[e, OWN : OWN + 1, :] for e in range(MATES)]
    best = tops[0]
    for v in tops[1:]:
        best = jnp.maximum(best, v)
    scales = [jnp.exp2(v - best) for v in tops]
    total = sum(scales[e] * shares[e, OWN + 1 : OWN + 2, :] for e in range(MATES))
    out = jnp.zeros((OWN, LATENT), F32)
    for e in range(MATES):
        out += spread(scales[e] / total) * shares[e, 0:OWN, :]
    out_ref[own_rows, :] = out

    def o_view(chunk, block):
        rows = OWN // O_CHUNKS
        return out_ref.at[pl.ds(pl.multiple_of(block * OWN + chunk * rows, rows), rows), :]

    for step in range(NTGT // 2 + 1):
        ring_step(o_view, or_send, or_recv, step, O_CHUNKS)

    for chunk in range(2):
        for way in range(2):
            n = hops(way, chunk)
            wait_bytes(tg.at[pl.ds(0, n), pl.ds(0, PIECE // 2), :], tr_send.at[way, chunk])
    for chunk in range(O_CHUNKS):
        for way in range(2):
            wait_bytes(out_ref.at[pl.ds(0, hops(way, chunk) * (OWN // O_CHUNKS)), :], or_send.at[way, chunk])
    wait_bytes(xs.at[pl.ds(0, MATES - 1)], xs_sem.at[0])
    wait_bytes(part.at[pl.ds(0, MATES - 1)], part_sem.at[0])
    for it in range(ITERS):
        wait_bytes(rs.at[it, pl.ds(0, NTGT - 1)], rs_sem.at[it, 0])
        wait_bytes(cr.at[it, pl.ds(0, NSRC - 1)], cr_sem.at[it, 0])
    wait_bytes(qg.at[pl.ds(0, NTGT - 1)], qg_sem.at[0])


def deliver(sp_in, tp_in, bary_in, sp_out, tp_out, bary_out, sems):
    rows = ROWS // DELIVERIES
    copies = [(sp_in, sp_out), (tp_in, tp_out)]
    for k in range(DELIVERIES):
        at = pl.ds(k * rows, rows)
        copies.append((bary_in.at[at, :], bary_out.at[at, :]))
    copies = [pltpu.make_async_copy(a, b, sems.at[k]) for k, (a, b) in enumerate(copies)]
    for copy in copies:
        copy.start()
    for copy in copies:
        copy.wait()


def on_device(sources, targets, log_source, log_target):
    vmem = pl.BlockSpec(memory_space=pltpu.VMEM)
    dma = pltpu.SemaphoreType.DMA
    sp, tp, bary = pl.pallas_call(
        kernel,
        out_shape=(
            jax.ShapeDtypeStruct((RCH, LANES), F32),
            jax.ShapeDtypeStruct((CCH, LANES), F32),
            jax.ShapeDtypeStruct((ROWS, LATENT), F32),
        ),
        in_specs=[vmem] * 4,
        out_specs=(vmem,) * 3,
        scratch_shapes=[
            pltpu.VMEM((3 * LATENT, ROWS), BF16),
            pltpu.VMEM((COLS, 3 * LATENT), BF16),
            pltpu.VMEM((COLS, ROWS), F32),
            pltpu.VMEM((MATES * OWN, NTGT * PIECE), F32),
            pltpu.VMEM((COLS, LANES), F32),
            pltpu.VMEM((RCH, LANES), F32),
            pltpu.VMEM((RCH, LANES), F32),
            pltpu.VMEM((CCH, LANES), F32),
            pltpu.VMEM((RCH, 8, LANES), F32),
            pltpu.VMEM((RCH, 8, LANES), F32),
            pltpu.VMEM((COLS, LANES), F32),
            pltpu.VMEM((COLS, LANES), F32),
            pltpu.VMEM((ITERS, RCH, LANES), F32),
            pltpu.VMEM((ITERS, NTGT, RCH, LANES), F32),
            pltpu.VMEM((ITERS, CCH, LANES), F32),
            pltpu.VMEM((ITERS, NSRC, CCH, LANES), F32),
            pltpu.VMEM((CCH, 1, LANES), F32),
            pltpu.VMEM((NTGT, 1, LANES), F32),
            pltpu.VMEM((NTGT, PIECE, LATENT), F32),
            pltpu.VMEM((MATES, OWN, LATENT), F32),
            pltpu.VMEM((MATES * OWN, 3 * LATENT), BF16),
            pltpu.VMEM((NTGT * PIECE, 2 * LATENT), BF16),
            pltpu.VMEM((2 * OWN, LANES), F32),
            pltpu.VMEM((2 * OWN, LANES), F32),
            pltpu.VMEM((2 * OWN, LATENT), F32),
            pltpu.VMEM((MATES, OWN + 8, LATENT), F32),
            pltpu.VMEM((MATES, OWN + 8, LATENT), F32),
            dma((ITERS, 2)),
            dma((ITERS, 2)),
            dma((2,)),
            dma((2, 2)), dma((2, 2, 8)),
            dma((2, O_CHUNKS)), dma((2, O_CHUNKS, 8)),
            dma((2,)),
            dma((2,)),
        ],
        compiler_params=pltpu.CompilerParams(
            collective_id=0, has_side_effects=True, vmem_limit_bytes=56 * 2**20
        ),
        cost_estimate=pl.CostEstimate(flops=6 * 10**9, bytes_accessed=4 * 2**20, transcendentals=10**7),
        name="coupling",
    )(
        sources,
        targets,
        log_source.reshape(RCH, LANES),
        log_target.reshape(CCH, LANES),
    )
    sp, tp, bary = pl.pallas_call(
        deliver,
        out_shape=tuple(jax.ShapeDtypeStruct(v.shape, F32) for v in (sp, tp, bary)),
        in_specs=[pl.BlockSpec(memory_space=pl.ANY)] * 3,
        out_specs=(pl.BlockSpec(memory_space=pl.ANY),) * 3,
        scratch_shapes=[dma((2 + DELIVERIES,))],
        name="deliver",
    )(sp, tp, bary)
    return sp.reshape(ROWS), tp.reshape(COLS), bary


def solution(mesh):
    in_specs = (P("src", None), P("tgt", None), P("src"), P("tgt"))
    out_specs = (P("src"), P("tgt"), P("src", None))
    return jax.shard_map(
        on_device, mesh=mesh, in_specs=in_specs, out_specs=out_specs, check_vma=False
    )
```

```python
import functools
import math

import jax
import jax.numpy as jnp
from jax import lax
from jax.experimental import pallas as pl
from jax.experimental.pallas import tpu as pltpu
from jax.sharding import PartitionSpec as P

ITERS = 2
LATENT = 128
LANES = 128
LOG2E = math.log2(math.e)
LN2 = math.log(2.0)
MESH = pl.DeviceIdType.MESH

NSRC, NTGT = 32, 16
GRID_X, GRID_Y = 4, 4
ROWS, COLS = 2048, 1024
RCH, CCH = ROWS // LANES, COLS // LANES
OWN = ROWS // NTGT
MATES = GRID_X * 2
PIECE = COLS // MATES
F32, BF16 = jnp.float32, jnp.bfloat16


def split3(v, order, axis=1):
    high = v.astype(BF16)
    low = (v - high.astype(F32)).astype(BF16)
    return jnp.concatenate([(high, low)[k] for k in order], axis=axis)


def dot(a, b):
    return jnp.dot(a, b, preferred_element_type=F32)


def spread(row):
    return jnp.broadcast_to(row, (LANES, LANES)).T


def lse_down(z_ref, b_ref, top_ref, total_ref):
    rows, cols = z_ref.shape
    width, depth = 2, 128

    @pl.loop(0, cols // (width * LANES))
    def _(col):
        def block(n, state):
            at = pl.ds(pl.multiple_of(n * depth, depth), depth)
            out = []
            for k in range(width):
                top, total = state[k]
                lane = pl.multiple_of(col * width * LANES + k * LANES, LANES)
                v = (z_ref[at, pl.ds(lane, LANES)] + b_ref[at, :]).reshape(depth // 8, 8, LANES)
                new = jnp.maximum(top, jnp.max(v, axis=0))
                total = total * jnp.exp2(top - new) + jnp.sum(jnp.exp2(v - new[None]), axis=0)
                out.append((new, total))
            return tuple(out)

        start = (jnp.full((8, LANES), -jnp.inf, F32), jnp.zeros((8, LANES), F32))
        state = lax.fori_loop(0, rows // depth, block, (start,) * width, unroll=True)
        for k in range(width):
            top_ref[col * width + k], total_ref[col * width + k] = state[k]

    tops = top_ref[...]
    best = jnp.max(tops, axis=1)
    total = jnp.sum(total_ref[...] * jnp.exp2(tops - best[:, None, :]), axis=1)
    return best + LOG2E * jnp.log(total)


def lse_across(z_ref, b_ref, top_ref, total_ref, out_ref):
    rows, cols = z_ref.shape
    depth = 16

    @pl.loop(0, rows // depth, unroll=4)
    def _(n):
        at = pl.ds(pl.multiple_of(n * depth, depth), depth)
        v = [z_ref[at, c * LANES : (c + 1) * LANES] + b_ref[c : c + 1, :] for c in range(cols // LANES)]
        top = functools.reduce(jnp.maximum, v)
        top_ref[at, :] = top
        total_ref[at, :] = sum(jnp.exp2(x - top) for x in v)

    for k in range(rows // LANES):
        at = slice(k * LANES, (k + 1) * LANES)
        top = top_ref[at, :].T
        best = jnp.max(top, axis=0, keepdims=True)
        total = jnp.sum(total_ref[at, :].T * jnp.exp2(top - best), axis=0, keepdims=True)
        out_ref[k : k + 1, :] = best + LOG2E * jnp.log(total)


def combine(parts):
    top = jnp.max(parts, axis=0)
    return top + LOG2E * jnp.log(jnp.sum(jnp.exp2(parts - top[None]), axis=0))


def kernel(
    x_ref, y_ref, la_ref, lb_ref, sp_ref, tp_ref, out_ref,
    xt, ya, zt, zf, qb, pv, nx, ny, top8, total8, tops, totals,
    l_row, rs, l_col, cr, qs, qg, tg, xs, xf, yf, mf, sf, acc, part, shares,
    rs_sem, cr_sem, qg_sem, tr_send, tr_recv, xs_sem, part_sem,
):
    s, t = lax.axis_index("src"), lax.axis_index("tgt")
    gx, gy, core = s // (GRID_Y * 2), lax.rem(s // 2, GRID_Y), lax.rem(s, 2)
    me = gx * 2 + core

    def z_peer(k):
        return lax.rem(t + k, NTGT)

    def s_peer(k):
        return lax.rem(s + k, NSRC)

    def mate(e):
        return ((e // 2) * GRID_Y + gy) * 2 + lax.rem(e, 2)

    barrier = pltpu.get_barrier_semaphore()

    @pl.loop(1, NTGT)
    def _(k):
        pl.semaphore_signal(barrier, inc=1, device_id=(s, z_peer(k)), device_id_type=MESH)

    @pl.loop(1, NSRC)
    def _(k):
        pl.semaphore_signal(barrier, inc=1, device_id=(s_peer(k), t), device_id_type=MESH)

    def remote(src, dst, send, recv, device):
        return pltpu.make_async_remote_copy(
            src_ref=src, dst_ref=dst, send_sem=send, recv_sem=recv, device_id=device, device_id_type=MESH
        )

    def wait_bytes(ref, sem):
        remote(ref, ref, sem, sem, (s, t)).wait_recv()

    @pl.loop(0, RCH, unroll=4)
    def _(k):
        at = pl.ds(pl.multiple_of(k * LANES, LANES), LANES)
        xt[:, at] = split3(x_ref[at, :].T * (2.0 * LOG2E), (0, 0, 1), axis=0)

    @pl.loop(0, CCH, unroll=2)
    def _(k):
        at = pl.ds(pl.multiple_of(k * LANES, LANES), LANES)
        y = y_ref[at, :]
        ya[at, :] = split3(y, (0, 1, 0))
        qb[at, :] = jnp.broadcast_to(-LOG2E * jnp.sum(y * y, axis=1, keepdims=True), (LANES, LANES))

    tg[t] = y_ref[pl.ds(pl.multiple_of(me * PIECE, PIECE), PIECE), :]
    own_rows = pl.ds(pl.multiple_of(t * OWN, OWN), OWN)
    xs[me] = x_ref[own_rows, :]

    @pl.loop(0, ROWS // 256)
    def _(k):
        at = pl.ds(pl.multiple_of(k * 256, 256), 256)
        zt[:, at] = dot(ya[...], xt[:, at])

    pl.semaphore_wait(barrier, NTGT - 1 + NSRC - 1)

    def hops(way, chunk):
        return NTGT // 2 - (way ^ chunk % 2)

    def ring_step(view, send, recv, step, chunks=2):
        for chunk in range(chunks):
            for way in range(2):
                if step > hops(way, chunk):
                    continue
                block = lax.rem(t + (NTGT - step if way == 0 else step), NTGT)
                ref = view(chunk, block)
                if step > 0:
                    wait_bytes(ref, recv.at[way, chunk, step - 1])
                if step < hops(way, chunk):
                    to = lax.rem(t + (1 if way == 0 else NTGT - 1), NTGT)
                    remote(ref, ref, send.at[way, chunk], recv.at[way, chunk, step], (s, to)).start()

    def t_view(chunk, block):
        return tg.at[block, pl.ds(chunk * (PIECE // 2), PIECE // 2), :]

    def t_step(step):
        ring_step(t_view, tr_send, tr_recv, step)

    t_step(0)

    @pl.loop(1, MATES)
    def _(k):
        to = mate(lax.rem(me + k, MATES))
        remote(xs.at[me], xs.at[me], xs_sem.at[0], xs_sem.at[1], (to, t)).start()

    def last_scores(first, last):
        @pl.loop(first, last)
        def _(b):
            at = pl.ds(pl.multiple_of(b * 2 * PIECE, 2 * PIECE), 2 * PIECE)
            y = tg[pl.ds(b * 2, 2)].reshape(2 * PIECE, LATENT)
            yf[at, :] = split3(y, (0, 1))
            zf[:, at] = dot(xf[...], split3(y.T, (0, 1, 0), axis=0))

    def last_rows(first, last):
        @pl.loop(first, last)
        def _(e):
            at = pl.ds(pl.multiple_of(e * OWN, OWN), OWN)
            xf[at, :] = split3(xs[e] * (2.0 * LOG2E), (0, 0, 1))

    for it in range(ITERS):
        l_row[it] = lse_down(zt, qb, top8, total8)

        @pl.loop(1, NTGT)
        def _(k):
            remote(l_row.at[it], rs.at[it, t], rs_sem.at[it, 0], rs_sem.at[it, 1], (s, z_peer(k))).start()

        rs[it, t] = l_row[it]
        if it == 0:
            t_step(1)
            for k in range(RCH):
                turned = x_ref[k * LANES : (k + 1) * LANES, :].T
                nx[k : k + 1, :] = jnp.sum(turned * turned, axis=0, keepdims=True)
            for k in range(CCH):
                turned = y_ref[k * LANES : (k + 1) * LANES, :].T
                ny[k : k + 1, :] = jnp.sum(turned * turned, axis=0, keepdims=True)
            t_step(2)
        else:
            t_step(8)
            last_scores(0, NTGT // 4)

        wait_bytes(rs.at[it, pl.ds(0, NTGT - 1)], rs_sem.at[it, 1])
        row_pot = LOG2E * la_ref[...] - combine(rs[it])
        pv[...] = row_pot
        if it == 0:
            t_step(3)
        lse_across(zt, pv, tops, totals, l_col.at[it])

        @pl.loop(1, NSRC)
        def _(k):
            remote(l_col.at[it], cr.at[it, s], cr_sem.at[it, 0], cr_sem.at[it, 1], (s_peer(k), t)).start()

        cr[it, s] = l_col[it]
        if it == 0:
            t_step(4)
            wait_bytes(xs.at[pl.ds(0, MATES - 1)], xs_sem.at[1])
            last_rows(0, MATES // 2)
            t_step(5)
            last_rows(MATES // 2, MATES)
            t_step(6)
        else:
            sp_ref[...] = row_pot * LN2 + nx[...]
            last_scores(NTGT // 4, NTGT // 2)

        wait_bytes(cr.at[it, pl.ds(0, NSRC - 1)], cr_sem.at[it, 1])
        q = LOG2E * lb_ref[...] - combine(cr[it])
        if it == 0:
            for k in range(CCH):
                qb[k * LANES : (k + 1) * LANES, :] = spread(q[k : k + 1, :])
            t_step(7)

    for k in range(CCH):
        qs[k] = q[k : k + 1, :]
    qg[t] = qs[me]

    @pl.loop(1, NTGT)
    def _(k):
        remote(qs.at[me], qg.at[t], qg_sem.at[0], qg_sem.at[1], (s, z_peer(k))).start()

    tp_ref[...] = q * LN2 + ny[...]
    wait_bytes(qg.at[pl.ds(0, NTGT - 1)], qg_sem.at[1])

    depth = 64
    for far in (2, 1, 3, 0):
        chip = lax.rem(gx + far, GRID_X)
        base = chip * 2 * OWN

        @pl.loop(0, 2 * OWN // depth)
        def _(r):
            at = pl.ds(pl.multiple_of(base + r * depth, depth), depth)
            best = zf[at, 0:LANES] + qg[0]
            for b in range(1, NTGT):
                best = jnp.maximum(best, zf[at, b * LANES : (b + 1) * LANES] + qg[b])
            to = pl.ds(pl.multiple_of(r * depth, depth), depth)
            mf[to, :] = jnp.broadcast_to(jnp.max(best, axis=1, keepdims=True), (depth, LANES))

        sf[...] = jnp.zeros_like(sf)
        acc[...] = jnp.zeros_like(acc)
        at = pl.ds(pl.multiple_of(base, 2 * OWN), 2 * OWN)
        group = 4

        @pl.loop(0, NTGT // group, unroll=2)
        def _(b):
            highs, lows = [], []
            total = sf[...]
            for k in range(group):
                lane = pl.ds(pl.multiple_of((b * group + k) * LANES, LANES), LANES)
                w = jnp.exp2(zf[at, lane] + qg[b * group + k] - mf[...])
                total += w
                high = w.astype(BF16)
                highs.append(high)
                lows.append((w - high.astype(F32)).astype(BF16))
            sf[...] = total
            ys = pl.ds(pl.multiple_of(b * group * LANES, group * LANES), group * LANES)
            both = jnp.dot(jnp.concatenate(highs, axis=1), yf[ys, 0 : 2 * LATENT], preferred_element_type=F32)
            rest = jnp.dot(jnp.concatenate(lows, axis=1), yf[ys, 0:LATENT], preferred_element_type=F32)
            acc[...] += both[:, :LATENT] + both[:, LATENT:] + rest

        for g in range(2):
            rows = slice(g * OWN, (g + 1) * OWN)
            to = chip * 2 + g
            part[to, 0:OWN, :] = acc[rows, :]
            part[to, OWN : OWN + 1, :] = mf[rows, :].T[0:1, :]
            part[to, OWN + 1 : OWN + 2, :] = jnp.sum(sf[rows, :].T, axis=0, keepdims=True)

            def send():
                remote(part.at[to], shares.at[me], part_sem.at[0], part_sem.at[1], (mate(to), t)).start()

            if far == 0:
                pl.when(core != g)(send)
            else:
                send()

    shares[me, 0 : OWN + 2, :] = part[me, 0 : OWN + 2, :]
    wait_bytes(shares.at[pl.ds(0, MATES - 1)], part_sem.at[1])
    tops = [shares[e, OWN : OWN + 1, :] for e in range(MATES)]
    best = tops[0]
    for v in tops[1:]:
        best = jnp.maximum(best, v)
    scales = [jnp.exp2(v - best) for v in tops]
    total = sum(scales[e] * shares[e, OWN + 1 : OWN + 2, :] for e in range(MATES))
    out = jnp.zeros((OWN, LATENT), F32)
    for e in range(MATES):
        out += spread(scales[e] / total) * shares[e, 0:OWN, :]
    out_ref[...] = out

    for chunk in range(2):
        for way in range(2):
            n = hops(way, chunk)
            wait_bytes(tg.at[pl.ds(0, n), pl.ds(0, PIECE // 2), :], tr_send.at[way, chunk])
    wait_bytes(xs.at[pl.ds(0, MATES - 1)], xs_sem.at[0])
    wait_bytes(part.at[pl.ds(0, MATES - 1)], part_sem.at[0])
    for it in range(ITERS):
        wait_bytes(rs.at[it, pl.ds(0, NTGT - 1)], rs_sem.at[it, 0])
        wait_bytes(cr.at[it, pl.ds(0, NSRC - 1)], cr_sem.at[it, 0])
    wait_bytes(qg.at[pl.ds(0, NTGT - 1)], qg_sem.at[0])


def on_device(sources, targets, log_source, log_target):
    vmem = pl.BlockSpec(memory_space=pltpu.VMEM)
    dma = pltpu.SemaphoreType.DMA
    sp, tp, bary = pl.pallas_call(
        kernel,
        out_shape=(
            jax.ShapeDtypeStruct((RCH, LANES), F32),
            jax.ShapeDtypeStruct((CCH, LANES), F32),
            jax.ShapeDtypeStruct((OWN, LATENT), F32),
        ),
        in_specs=[vmem] * 4,
        out_specs=(vmem,) * 3,
        scratch_shapes=[
            pltpu.VMEM((3 * LATENT, ROWS), BF16),
            pltpu.VMEM((COLS, 3 * LATENT), BF16),
            pltpu.VMEM((COLS, ROWS), F32),
            pltpu.VMEM((MATES * OWN, NTGT * PIECE), F32),
            pltpu.VMEM((COLS, LANES), F32),
            pltpu.VMEM((RCH, LANES), F32),
            pltpu.VMEM((RCH, LANES), F32),
            pltpu.VMEM((CCH, LANES), F32),
            pltpu.VMEM((RCH, 8, LANES), F32),
            pltpu.VMEM((RCH, 8, LANES), F32),
            pltpu.VMEM((COLS, LANES), F32),
            pltpu.VMEM((COLS, LANES), F32),
            pltpu.VMEM((ITERS, RCH, LANES), F32),
            pltpu.VMEM((ITERS, NTGT, RCH, LANES), F32),
            pltpu.VMEM((ITERS, CCH, LANES), F32),
            pltpu.VMEM((ITERS, NSRC, CCH, LANES), F32),
            pltpu.VMEM((CCH, 1, LANES), F32),
            pltpu.VMEM((NTGT, 1, LANES), F32),
            pltpu.VMEM((NTGT, PIECE, LATENT), F32),
            pltpu.VMEM((MATES, OWN, LATENT), F32),
            pltpu.VMEM((MATES * OWN, 3 * LATENT), BF16),
            pltpu.VMEM((NTGT * PIECE, 2 * LATENT), BF16),
            pltpu.VMEM((2 * OWN, LANES), F32),
            pltpu.VMEM((2 * OWN, LANES), F32),
            pltpu.VMEM((2 * OWN, LATENT), F32),
            pltpu.VMEM((MATES, OWN + 8, LATENT), F32),
            pltpu.VMEM((MATES, OWN + 8, LATENT), F32),
            dma((ITERS, 2)),
            dma((ITERS, 2)),
            dma((2,)),
            dma((2, 2)), dma((2, 2, 8)),
            dma((2,)),
            dma((2,)),
        ],
        compiler_params=pltpu.CompilerParams(
            collective_id=0, has_side_effects=True, vmem_limit_bytes=56 * 2**20
        ),
        cost_estimate=pl.CostEstimate(flops=6 * 10**9, bytes_accessed=4 * 2**20, transcendentals=10**7),
        name="coupling",
    )(
        sources,
        targets,
        log_source.reshape(RCH, LANES),
        log_target.reshape(CCH, LANES),
    )
    bary = lax.all_gather(bary, "tgt", axis=0, tiled=True)
    return sp.reshape(ROWS), tp.reshape(COLS), bary


def solution(mesh):
    in_specs = (P("src", None), P("tgt", None), P("src"), P("tgt"))
    out_specs = (P("src"), P("tgt"), P("src", None))
    return jax.shard_map(
        on_device, mesh=mesh, in_specs=in_specs, out_specs=out_specs, check_vma=False
    )
```

```python
import functools
import math

import jax
import jax.numpy as jnp
from jax import lax
from jax.experimental import pallas as pl
from jax.experimental.pallas import tpu as pltpu
from jax.sharding import PartitionSpec as P

ITERS = 2
LATENT = 128
LANES = 128
LOG2E = math.log2(math.e)
LN2 = math.log(2.0)
MESH = pl.DeviceIdType.MESH

NSRC, NTGT = 32, 16
GRID_X, GRID_Y = 4, 4
ROWS, COLS = 2048, 1024
RCH, CCH = ROWS // LANES, COLS // LANES
OWN = ROWS // NTGT
O_CHUNKS = 2
MATES = GRID_X * 2
DELIVERIES = 4
PIECE = COLS // MATES
F32, BF16 = jnp.float32, jnp.bfloat16


def split3(v, order, axis=1):
    high = v.astype(BF16)
    low = (v - high.astype(F32)).astype(BF16)
    return jnp.concatenate([(high, low)[k] for k in order], axis=axis)


def dot(a, b):
    return jnp.dot(a, b, preferred_element_type=F32)


def spread(row):
    return jnp.broadcast_to(row, (LANES, LANES)).T


def lse_down(z_ref, b_ref, top_ref, total_ref):
    rows, cols = z_ref.shape
    width, depth = 2, 128

    @pl.loop(0, cols // (width * LANES))
    def _(col):
        def block(n, state):
            at = pl.ds(pl.multiple_of(n * depth, depth), depth)
            out = []
            for k in range(width):
                top, total = state[k]
                lane = pl.multiple_of(col * width * LANES + k * LANES, LANES)
                v = (z_ref[at, pl.ds(lane, LANES)] + b_ref[at, :]).reshape(depth // 8, 8, LANES)
                new = jnp.maximum(top, jnp.max(v, axis=0))
                total = total * jnp.exp2(top - new) + jnp.sum(jnp.exp2(v - new[None]), axis=0)
                out.append((new, total))
            return tuple(out)

        start = (jnp.full((8, LANES), -jnp.inf, F32), jnp.zeros((8, LANES), F32))
        state = lax.fori_loop(0, rows // depth, block, (start,) * width, unroll=True)
        for k in range(width):
            top_ref[col * width + k], total_ref[col * width + k] = state[k]

    tops = top_ref[...]
    best = jnp.max(tops, axis=1)
    total = jnp.sum(total_ref[...] * jnp.exp2(tops - best[:, None, :]), axis=1)
    return best + LOG2E * jnp.log(total)


def lse_across(z_ref, b_ref, top_ref, total_ref, out_ref):
    rows, cols = z_ref.shape
    depth = 16

    @pl.loop(0, rows // depth, unroll=4)
    def _(n):
        at = pl.ds(pl.multiple_of(n * depth, depth), depth)
        v = [z_ref[at, c * LANES : (c + 1) * LANES] + b_ref[c : c + 1, :] for c in range(cols // LANES)]
        top = functools.reduce(jnp.maximum, v)
        top_ref[at, :] = top
        total_ref[at, :] = sum(jnp.exp2(x - top) for x in v)

    for k in range(rows // LANES):
        at = slice(k * LANES, (k + 1) * LANES)
        top = top_ref[at, :].T
        best = jnp.max(top, axis=0, keepdims=True)
        total = jnp.sum(total_ref[at, :].T * jnp.exp2(top - best), axis=0, keepdims=True)
        out_ref[k : k + 1, :] = best + LOG2E * jnp.log(total)


def combine(parts):
    top = jnp.max(parts, axis=0)
    return top + LOG2E * jnp.log(jnp.sum(jnp.exp2(parts - top[None]), axis=0))


def kernel(
    x_ref, y_ref, la_ref, lb_ref, sp_ref, tp_ref, out_ref,
    xt, ya, zt, zf, qb, pv, nx, ny, top8, total8, tops, totals,
    l_row, rs, l_col, cr, qs, qg, tg, xs, xf, yf, mf, sf, acc, part, shares,
    rs_sem, cr_sem, qg_sem, tr_send, tr_recv, or_send, or_recv, xs_sem, part_sem,
):
    s, t = lax.axis_index("src"), lax.axis_index("tgt")
    gx, gy, core = s // (GRID_Y * 2), lax.rem(s // 2, GRID_Y), lax.rem(s, 2)
    me = gx * 2 + core

    def z_peer(k):
        return lax.rem(t + k, NTGT)

    def s_peer(k):
        return lax.rem(s + k, NSRC)

    def mate(e):
        return ((e // 2) * GRID_Y + gy) * 2 + lax.rem(e, 2)

    barrier = pltpu.get_barrier_semaphore()

    @pl.loop(1, NTGT)
    def _(k):
        pl.semaphore_signal(barrier, inc=1, device_id=(s, z_peer(k)), device_id_type=MESH)

    @pl.loop(1, NSRC)
    def _(k):
        pl.semaphore_signal(barrier, inc=1, device_id=(s_peer(k), t), device_id_type=MESH)

    def remote(src, dst, send, recv, device):
        return pltpu.make_async_remote_copy(
            src_ref=src, dst_ref=dst, send_sem=send, recv_sem=recv, device_id=device, device_id_type=MESH
        )

    def wait_bytes(ref, sem):
        remote(ref, ref, sem, sem, (s, t)).wait_recv()

    @pl.loop(0, RCH, unroll=4)
    def _(k):
        at = pl.ds(pl.multiple_of(k * LANES, LANES), LANES)
        xt[:, at] = split3(x_ref[at, :].T * (2.0 * LOG2E), (0, 0, 1), axis=0)

    @pl.loop(0, CCH, unroll=2)
    def _(k):
        at = pl.ds(pl.multiple_of(k * LANES, LANES), LANES)
        y = y_ref[at, :]
        ya[at, :] = split3(y, (0, 1, 0))
        qb[at, :] = jnp.broadcast_to(-LOG2E * jnp.sum(y * y, axis=1, keepdims=True), (LANES, LANES))

    tg[t] = y_ref[pl.ds(pl.multiple_of(me * PIECE, PIECE), PIECE), :]
    own_rows = pl.ds(pl.multiple_of(t * OWN, OWN), OWN)
    xs[me] = x_ref[own_rows, :]

    @pl.loop(0, ROWS // 256)
    def _(k):
        at = pl.ds(pl.multiple_of(k * 256, 256), 256)
        zt[:, at] = dot(ya[...], xt[:, at])

    pl.semaphore_wait(barrier, NTGT - 1 + NSRC - 1)

    def reach(way, chunk):
        return NTGT // 2 - (way ^ chunk % 2)

    def away(way, distance):
        return lax.rem(t + (distance if way == 0 else NTGT - distance), NTGT)

    def ring_wait(view, recv, way, chunk, distance):
        ref = view(chunk, away(1 - way, distance))
        wait_bytes(ref, recv.at[way, chunk, distance - 1])

    def ring_step(view, send, recv, distance, chunks=2):
        for chunk in range(chunks):
            for way in range(2):
                if distance > 0:
                    ring_wait(view, recv, way, chunk, distance)
                ref = view(chunk, away(1 - way, distance))
                for stride in (2, 1):
                    there = distance + stride
                    if there <= reach(way, chunk):
                        at = recv.at[way, chunk, there - 1]
                        remote(ref, ref, send.at[way, chunk], at, (s, away(way, stride))).start()

    def ring_end(view, recv, chunks=2):
        for distance in (1, 3, 5, 7, 8):
            for chunk in range(chunks):
                for way in range(2):
                    if distance <= reach(way, chunk):
                        ring_wait(view, recv, way, chunk, distance)

    def t_view(chunk, block):
        return tg.at[block, pl.ds(chunk * (PIECE // 2), PIECE // 2), :]

    def t_step(step):
        ring_step(t_view, tr_send, tr_recv, step)

    t_step(0)

    @pl.loop(1, MATES)
    def _(k):
        to = mate(lax.rem(me + k, MATES))
        remote(xs.at[me], xs.at[me], xs_sem.at[0], xs_sem.at[1], (to, t)).start()

    def last_scores(first, last):
        @pl.loop(first, last)
        def _(b):
            at = pl.ds(pl.multiple_of(b * 2 * PIECE, 2 * PIECE), 2 * PIECE)
            y = tg[pl.ds(b * 2, 2)].reshape(2 * PIECE, LATENT)
            yf[at, :] = split3(y, (0, 1))
            zf[:, at] = dot(xf[...], split3(y.T, (0, 1, 0), axis=0))

    def last_rows(first, last):
        @pl.loop(first, last)
        def _(e):
            at = pl.ds(pl.multiple_of(e * OWN, OWN), OWN)
            xf[at, :] = split3(xs[e] * (2.0 * LOG2E), (0, 0, 1))

    for it in range(ITERS):
        l_row[it] = lse_down(zt, qb, top8, total8)

        @pl.loop(1, NTGT)
        def _(k):
            remote(l_row.at[it], rs.at[it, t], rs_sem.at[it, 0], rs_sem.at[it, 1], (s, z_peer(k))).start()

        rs[it, t] = l_row[it]
        if it == 0:
            t_step(2)
            for k in range(RCH):
                turned = x_ref[k * LANES : (k + 1) * LANES, :].T
                nx[k : k + 1, :] = jnp.sum(turned * turned, axis=0, keepdims=True)
            for k in range(CCH):
                turned = y_ref[k * LANES : (k + 1) * LANES, :].T
                ny[k : k + 1, :] = jnp.sum(turned * turned, axis=0, keepdims=True)
        else:
            ring_end(t_view, tr_recv)
            last_scores(0, NTGT // 4)

        wait_bytes(rs.at[it, pl.ds(0, NTGT - 1)], rs_sem.at[it, 1])
        row_pot = LOG2E * la_ref[...] - combine(rs[it])
        pv[...] = row_pot
        if it == 0:
            t_step(4)
        lse_across(zt, pv, tops, totals, l_col.at[it])

        @pl.loop(1, NSRC)
        def _(k):
            remote(l_col.at[it], cr.at[it, s], cr_sem.at[it, 0], cr_sem.at[it, 1], (s_peer(k), t)).start()

        cr[it, s] = l_col[it]
        if it == 0:
            wait_bytes(xs.at[pl.ds(0, MATES - 1)], xs_sem.at[1])
            last_rows(0, MATES)
            t_step(6)
        else:
            sp_ref[...] = row_pot * LN2 + nx[...]
            last_scores(NTGT // 4, NTGT // 2)

        wait_bytes(cr.at[it, pl.ds(0, NSRC - 1)], cr_sem.at[it, 1])
        q = LOG2E * lb_ref[...] - combine(cr[it])
        if it == 0:
            for k in range(CCH):
                qb[k * LANES : (k + 1) * LANES, :] = spread(q[k : k + 1, :])

    for k in range(CCH):
        qs[k] = q[k : k + 1, :]
    qg[t] = qs[me]

    @pl.loop(1, NTGT)
    def _(k):
        remote(qs.at[me], qg.at[t], qg_sem.at[0], qg_sem.at[1], (s, z_peer(k))).start()

    tp_ref[...] = q * LN2 + ny[...]
    wait_bytes(qg.at[pl.ds(0, NTGT - 1)], qg_sem.at[1])

    depth = 64
    for far in (2, 1, 3, 0):
        chip = lax.rem(gx + far, GRID_X)
        base = chip * 2 * OWN

        @pl.loop(0, 2 * OWN // depth)
        def _(r):
            at = pl.ds(pl.multiple_of(base + r * depth, depth), depth)
            best = zf[at, 0:LANES] + qg[0]
            for b in range(1, NTGT):
                best = jnp.maximum(best, zf[at, b * LANES : (b + 1) * LANES] + qg[b])
            to = pl.ds(pl.multiple_of(r * depth, depth), depth)
            mf[to, :] = jnp.broadcast_to(jnp.max(best, axis=1, keepdims=True), (depth, LANES))

        sf[...] = jnp.zeros_like(sf)
        acc[...] = jnp.zeros_like(acc)
        at = pl.ds(pl.multiple_of(base, 2 * OWN), 2 * OWN)
        group = 4

        @pl.loop(0, NTGT // group, unroll=2)
        def _(b):
            highs, lows = [], []
            total = sf[...]
            for k in range(group):
                lane = pl.ds(pl.multiple_of((b * group + k) * LANES, LANES), LANES)
                w = jnp.exp2(zf[at, lane] + qg[b * group + k] - mf[...])
                total += w
                high = w.astype(BF16)
                highs.append(high)
                lows.append((w - high.astype(F32)).astype(BF16))
            sf[...] = total
            ys = pl.ds(pl.multiple_of(b * group * LANES, group * LANES), group * LANES)
            both = jnp.dot(jnp.concatenate(highs, axis=1), yf[ys, 0 : 2 * LATENT], preferred_element_type=F32)
            rest = jnp.dot(jnp.concatenate(lows, axis=1), yf[ys, 0:LATENT], preferred_element_type=F32)
            acc[...] += both[:, :LATENT] + both[:, LATENT:] + rest

        for g in range(2):
            rows = slice(g * OWN, (g + 1) * OWN)
            to = chip * 2 + g
            part[to, 0:OWN, :] = acc[rows, :]
            part[to, OWN : OWN + 1, :] = mf[rows, :].T[0:1, :]
            part[to, OWN + 1 : OWN + 2, :] = jnp.sum(sf[rows, :].T, axis=0, keepdims=True)

            def send():
                remote(part.at[to], shares.at[me], part_sem.at[0], part_sem.at[1], (mate(to), t)).start()

            if far == 0:
                pl.when(core != g)(send)
            else:
                send()

    shares[me, 0 : OWN + 2, :] = part[me, 0 : OWN + 2, :]
    wait_bytes(shares.at[pl.ds(0, MATES - 1)], part_sem.at[1])
    tops = [shares[e, OWN : OWN + 1, :] for e in range(MATES)]
    best = tops[0]
    for v in tops[1:]:
        best = jnp.maximum(best, v)
    scales = [jnp.exp2(v - best) for v in tops]
    total = sum(scales[e] * shares[e, OWN + 1 : OWN + 2, :] for e in range(MATES))
    out = jnp.zeros((OWN, LATENT), F32)
    for e in range(MATES):
        out += spread(scales[e] / total) * shares[e, 0:OWN, :]
    out_ref[own_rows, :] = out

    def o_view(chunk, block):
        rows = OWN // O_CHUNKS
        return out_ref.at[pl.ds(pl.multiple_of(block * OWN + chunk * rows, rows), rows), :]

    for distance in range(0, NTGT // 2, 2):
        ring_step(o_view, or_send, or_recv, distance, O_CHUNKS)
    ring_end(o_view, or_recv, O_CHUNKS)

    for chunk in range(2):
        for way in range(2):
            n = reach(way, chunk)
            wait_bytes(tg.at[pl.ds(0, n), pl.ds(0, PIECE // 2), :], tr_send.at[way, chunk])
    for chunk in range(O_CHUNKS):
        for way in range(2):
            wait_bytes(out_ref.at[pl.ds(0, reach(way, chunk) * (OWN // O_CHUNKS)), :], or_send.at[way, chunk])
    wait_bytes(xs.at[pl.ds(0, MATES - 1)], xs_sem.at[0])
    wait_bytes(part.at[pl.ds(0, MATES - 1)], part_sem.at[0])
    for it in range(ITERS):
        wait_bytes(rs.at[it, pl.ds(0, NTGT - 1)], rs_sem.at[it, 0])
        wait_bytes(cr.at[it, pl.ds(0, NSRC - 1)], cr_sem.at[it, 0])
    wait_bytes(qg.at[pl.ds(0, NTGT - 1)], qg_sem.at[0])


def deliver(sp_in, tp_in, bary_in, sp_out, tp_out, bary_out):
    sp_out[...] = sp_in[...]
    tp_out[...] = tp_in[...]
    bary_out[...] = bary_in[...]


def on_device(sources, targets, log_source, log_target):
    vmem = pl.BlockSpec(memory_space=pltpu.VMEM)
    dma = pltpu.SemaphoreType.DMA
    sp, tp, bary = pl.pallas_call(
        kernel,
        out_shape=(
            jax.ShapeDtypeStruct((RCH, LANES), F32),
            jax.ShapeDtypeStruct((CCH, LANES), F32),
            jax.ShapeDtypeStruct((ROWS, LATENT), F32),
        ),
        in_specs=[vmem] * 4,
        out_specs=(vmem,) * 3,
        scratch_shapes=[
            pltpu.VMEM((3 * LATENT, ROWS), BF16),
            pltpu.VMEM((COLS, 3 * LATENT), BF16),
            pltpu.VMEM((COLS, ROWS), F32),
            pltpu.VMEM((MATES * OWN, NTGT * PIECE), F32),
            pltpu.VMEM((COLS, LANES), F32),
            pltpu.VMEM((RCH, LANES), F32),
            pltpu.VMEM((RCH, LANES), F32),
            pltpu.VMEM((CCH, LANES), F32),
            pltpu.VMEM((RCH, 8, LANES), F32),
            pltpu.VMEM((RCH, 8, LANES), F32),
            pltpu.VMEM((COLS, LANES), F32),
            pltpu.VMEM((COLS, LANES), F32),
            pltpu.VMEM((ITERS, RCH, LANES), F32),
            pltpu.VMEM((ITERS, NTGT, RCH, LANES), F32),
            pltpu.VMEM((ITERS, CCH, LANES), F32),
            pltpu.VMEM((ITERS, NSRC, CCH, LANES), F32),
            pltpu.VMEM((CCH, 1, LANES), F32),
            pltpu.VMEM((NTGT, 1, LANES), F32),
            pltpu.VMEM((NTGT, PIECE, LATENT), F32),
            pltpu.VMEM((MATES, OWN, LATENT), F32),
            pltpu.VMEM((MATES * OWN, 3 * LATENT), BF16),
            pltpu.VMEM((NTGT * PIECE, 2 * LATENT), BF16),
            pltpu.VMEM((2 * OWN, LANES), F32),
            pltpu.VMEM((2 * OWN, LANES), F32),
            pltpu.VMEM((2 * OWN, LATENT), F32),
            pltpu.VMEM((MATES, OWN + 8, LATENT), F32),
            pltpu.VMEM((MATES, OWN + 8, LATENT), F32),
            dma((ITERS, 2)),
            dma((ITERS, 2)),
            dma((2,)),
            dma((2, 2)), dma((2, 2, 8)),
            dma((2, O_CHUNKS)), dma((2, O_CHUNKS, 8)),
            dma((2,)),
            dma((2,)),
        ],
        compiler_params=pltpu.CompilerParams(
            collective_id=0, has_side_effects=True, vmem_limit_bytes=56 * 2**20
        ),
        cost_estimate=pl.CostEstimate(flops=6 * 10**9, bytes_accessed=4 * 2**20, transcendentals=10**7),
        name="coupling",
    )(
        sources,
        targets,
        log_source.reshape(RCH, LANES),
        log_target.reshape(CCH, LANES),
    )
    blocks = [
        pl.BlockSpec((RCH, LANES), lambda k: (0, 0)),
        pl.BlockSpec((CCH, LANES), lambda k: (0, 0)),
        pl.BlockSpec((ROWS // DELIVERIES, LATENT), lambda k: (k, 0)),
    ]
    sp, tp, bary = pl.pallas_call(
        deliver,
        out_shape=tuple(jax.ShapeDtypeStruct(v.shape, F32) for v in (sp, tp, bary)),
        grid=(DELIVERIES,),
        in_specs=blocks,
        out_specs=tuple(blocks),
        name="deliver",
    )(sp, tp, bary)
    return sp.reshape(ROWS), tp.reshape(COLS), bary


def solution(mesh):
    in_specs = (P("src", None), P("tgt", None), P("src"), P("tgt"))
    out_specs = (P("src"), P("tgt"), P("src", None))
    return jax.shard_map(
        on_device, mesh=mesh, in_specs=in_specs, out_specs=out_specs, check_vma=False
    )
```

```python
import functools
import math

import jax
import jax.numpy as jnp
from jax import lax
from jax.experimental import pallas as pl
from jax.experimental.pallas import tpu as pltpu
from jax.sharding import PartitionSpec as P

ITERS = 2
LATENT = 128
LANES = 128
LOG2E = math.log2(math.e)
LN2 = math.log(2.0)
MESH = pl.DeviceIdType.MESH

NSRC, NTGT = 32, 16
GRID_X, GRID_Y = 4, 4
ROWS, COLS = 2048, 1024
RCH, CCH = ROWS // LANES, COLS // LANES
OWN = ROWS // NTGT
O_CHUNKS = 2
MATES = GRID_X * 2
DELIVERIES = 4
PIECE = COLS // MATES
F32, BF16 = jnp.float32, jnp.bfloat16


def split3(v, order, axis=1):
    high = v.astype(BF16)
    low = (v - high.astype(F32)).astype(BF16)
    return jnp.concatenate([(high, low)[k] for k in order], axis=axis)


def dot(a, b):
    return jnp.dot(a, b, preferred_element_type=F32)


def spread(row):
    return jnp.broadcast_to(row, (LANES, LANES)).T


def lse_down(z_ref, b_ref, top_ref, total_ref):
    rows, cols = z_ref.shape
    width, depth = 2, 128

    @pl.loop(0, cols // (width * LANES))
    def _(col):
        def block(n, state):
            at = pl.ds(pl.multiple_of(n * depth, depth), depth)
            out = []
            for k in range(width):
                top, total = state[k]
                lane = pl.multiple_of(col * width * LANES + k * LANES, LANES)
                v = (z_ref[at, pl.ds(lane, LANES)] + b_ref[at, :]).reshape(depth // 8, 8, LANES)
                new = jnp.maximum(top, jnp.max(v, axis=0))
                total = total * jnp.exp2(top - new) + jnp.sum(jnp.exp2(v - new[None]), axis=0)
                out.append((new, total))
            return tuple(out)

        start = (jnp.full((8, LANES), -jnp.inf, F32), jnp.zeros((8, LANES), F32))
        state = lax.fori_loop(0, rows // depth, block, (start,) * width, unroll=True)
        for k in range(width):
            top_ref[col * width + k], total_ref[col * width + k] = state[k]

    tops = top_ref[...]
    best = jnp.max(tops, axis=1)
    total = jnp.sum(total_ref[...] * jnp.exp2(tops - best[:, None, :]), axis=1)
    return best + LOG2E * jnp.log(total)


def lse_across(z_ref, b_ref, top_ref, total_ref, out_ref):
    rows, cols = z_ref.shape
    depth = 16

    @pl.loop(0, rows // depth, unroll=4)
    def _(n):
        at = pl.ds(pl.multiple_of(n * depth, depth), depth)
        v = [z_ref[at, c * LANES : (c + 1) * LANES] + b_ref[c : c + 1, :] for c in range(cols // LANES)]
        top = functools.reduce(jnp.maximum, v)
        top_ref[at, :] = top
        total_ref[at, :] = sum(jnp.exp2(x - top) for x in v)

    for k in range(rows // LANES):
        at = slice(k * LANES, (k + 1) * LANES)
        top = top_ref[at, :].T
        best = jnp.max(top, axis=0, keepdims=True)
        total = jnp.sum(total_ref[at, :].T * jnp.exp2(top - best), axis=0, keepdims=True)
        out_ref[k : k + 1, :] = best + LOG2E * jnp.log(total)


def combine(parts):
    top = jnp.max(parts, axis=0)
    return top + LOG2E * jnp.log(jnp.sum(jnp.exp2(parts - top[None]), axis=0))


def kernel(
    x_ref, y_ref, la_ref, lb_ref, sp_ref, tp_ref, out_ref,
    xt, ya, zt, zf, qb, pv, nx, ny, top8, total8, tops, totals,
    l_row, rs, l_col, cr, qs, qg, tg, xs, xf, yf, mf, sf, acc, part, shares,
    rs_sem, cr_sem, qg_sem, tr_send, tr_recv, or_send, or_recv, xs_sem, part_sem,
):
    s, t = lax.axis_index("src"), lax.axis_index("tgt")
    gx, gy, core = s // (GRID_Y * 2), lax.rem(s // 2, GRID_Y), lax.rem(s, 2)
    me = gx * 2 + core

    def z_peer(k):
        return lax.rem(t + k, NTGT)

    def s_peer(k):
        return lax.rem(s + k, NSRC)

    def mate(e):
        return ((e // 2) * GRID_Y + gy) * 2 + lax.rem(e, 2)

    barrier = pltpu.get_barrier_semaphore()

    @pl.loop(1, NTGT)
    def _(k):
        pl.semaphore_signal(barrier, inc=1, device_id=(s, z_peer(k)), device_id_type=MESH)

    @pl.loop(1, NSRC)
    def _(k):
        pl.semaphore_signal(barrier, inc=1, device_id=(s_peer(k), t), device_id_type=MESH)

    def remote(src, dst, send, recv, device):
        return pltpu.make_async_remote_copy(
            src_ref=src, dst_ref=dst, send_sem=send, recv_sem=recv, device_id=device, device_id_type=MESH
        )

    def wait_bytes(ref, sem):
        remote(ref, ref, sem, sem, (s, t)).wait_recv()

    @pl.loop(0, RCH, unroll=4)
    def _(k):
        at = pl.ds(pl.multiple_of(k * LANES, LANES), LANES)
        xt[:, at] = split3(x_ref[at, :].T * (2.0 * LOG2E), (0, 0, 1), axis=0)

    @pl.loop(0, CCH, unroll=2)
    def _(k):
        at = pl.ds(pl.multiple_of(k * LANES, LANES), LANES)
        y = y_ref[at, :]
        ya[at, :] = split3(y, (0, 1, 0))
        qb[at, :] = jnp.broadcast_to(-LOG2E * jnp.sum(y * y, axis=1, keepdims=True), (LANES, LANES))

    tg[t] = y_ref[pl.ds(pl.multiple_of(me * PIECE, PIECE), PIECE), :]
    own_rows = pl.ds(pl.multiple_of(t * OWN, OWN), OWN)
    xs[me] = x_ref[own_rows, :]

    @pl.loop(0, ROWS // 256)
    def _(k):
        at = pl.ds(pl.multiple_of(k * 256, 256), 256)
        zt[:, at] = dot(ya[...], xt[:, at])

    pl.semaphore_wait(barrier, NTGT - 1 + NSRC - 1)

    def reach(way, chunk):
        return NTGT // 2 - (way ^ chunk % 2)

    def away(way, distance):
        return lax.rem(t + (distance if way == 0 else NTGT - distance), NTGT)

    def ring_wait(view, recv, way, chunk, distance):
        ref = view(chunk, away(1 - way, distance))
        wait_bytes(ref, recv.at[way, chunk, distance - 1])

    def ring_step(view, send, recv, distance, chunks=2):
        for chunk in range(chunks):
            for way in range(2):
                if distance > 0:
                    ring_wait(view, recv, way, chunk, distance)
                ref = view(chunk, away(1 - way, distance))
                for stride in (2, 1):
                    there = distance + stride
                    if there <= reach(way, chunk):
                        at = recv.at[way, chunk, there - 1]
                        remote(ref, ref, send.at[way, chunk], at, (s, away(way, stride))).start()

    def ring_end(view, recv, chunks=2):
        for distance in (1, 3, 5, 7, 8):
            for chunk in range(chunks):
                for way in range(2):
                    if distance <= reach(way, chunk):
                        ring_wait(view, recv, way, chunk, distance)

    def t_view(chunk, block):
        return tg.at[block, pl.ds(chunk * (PIECE // 2), PIECE // 2), :]

    def t_step(step):
        ring_step(t_view, tr_send, tr_recv, step)

    t_step(0)

    @pl.loop(1, MATES)
    def _(k):
        to = mate(lax.rem(me + k, MATES))
        remote(xs.at[me], xs.at[me], xs_sem.at[0], xs_sem.at[1], (to, t)).start()

    def last_scores(first, last):
        @pl.loop(first, last)
        def _(b):
            at = pl.ds(pl.multiple_of(b * 2 * PIECE, 2 * PIECE), 2 * PIECE)
            y = tg[pl.ds(b * 2, 2)].reshape(2 * PIECE, LATENT)
            yf[at, :] = split3(y, (0, 1))
            zf[:, at] = dot(xf[...], split3(y.T, (0, 1, 0), axis=0))

    def last_rows(first, last):
        @pl.loop(first, last)
        def _(e):
            at = pl.ds(pl.multiple_of(e * OWN, OWN), OWN)
            xf[at, :] = split3(xs[e] * (2.0 * LOG2E), (0, 0, 1))

    for it in range(ITERS):
        l_row[it] = lse_down(zt, qb, top8, total8)

        @pl.loop(1, NTGT)
        def _(k):
            remote(l_row.at[it], rs.at[it, t], rs_sem.at[it, 0], rs_sem.at[it, 1], (s, z_peer(k))).start()

        rs[it, t] = l_row[it]
        if it == 0:
            for k in range(RCH):
                turned = x_ref[k * LANES : (k + 1) * LANES, :].T
                nx[k : k + 1, :] = jnp.sum(turned * turned, axis=0, keepdims=True)
            for k in range(CCH):
                turned = y_ref[k * LANES : (k + 1) * LANES, :].T
                ny[k : k + 1, :] = jnp.sum(turned * turned, axis=0, keepdims=True)
        else:
            ring_end(t_view, tr_recv)
            last_scores(0, NTGT // 4)

        wait_bytes(rs.at[it, pl.ds(0, NTGT - 1)], rs_sem.at[it, 1])
        row_pot = LOG2E * la_ref[...] - combine(rs[it])
        pv[...] = row_pot
        lse_across(zt, pv, tops, totals, l_col.at[it])

        @pl.loop(1, NSRC)
        def _(k):
            remote(l_col.at[it], cr.at[it, s], cr_sem.at[it, 0], cr_sem.at[it, 1], (s_peer(k), t)).start()

        cr[it, s] = l_col[it]
        if it == 0:
            t_step(2)
            wait_bytes(xs.at[pl.ds(0, MATES - 1)], xs_sem.at[1])
            last_rows(0, MATES)
            t_step(4)
        else:
            sp_ref[...] = row_pot * LN2 + nx[...]
            last_scores(NTGT // 4, NTGT // 2)

        wait_bytes(cr.at[it, pl.ds(0, NSRC - 1)], cr_sem.at[it, 1])
        q = LOG2E * lb_ref[...] - combine(cr[it])
        if it == 0:
            for k in range(CCH):
                qb[k * LANES : (k + 1) * LANES, :] = spread(q[k : k + 1, :])
            t_step(6)

    for k in range(CCH):
        qs[k] = q[k : k + 1, :]
    qg[t] = qs[me]

    @pl.loop(1, NTGT)
    def _(k):
        remote(qs.at[me], qg.at[t], qg_sem.at[0], qg_sem.at[1], (s, z_peer(k))).start()

    tp_ref[...] = q * LN2 + ny[...]
    wait_bytes(qg.at[pl.ds(0, NTGT - 1)], qg_sem.at[1])

    depth = 64
    for far in (2, 1, 3, 0):
        chip = lax.rem(gx + far, GRID_X)
        base = chip * 2 * OWN

        @pl.loop(0, 2 * OWN // depth)
        def _(r):
            at = pl.ds(pl.multiple_of(base + r * depth, depth), depth)
            best = zf[at, 0:LANES] + qg[0]
            for b in range(1, NTGT):
                best = jnp.maximum(best, zf[at, b * LANES : (b + 1) * LANES] + qg[b])
            to = pl.ds(pl.multiple_of(r * depth, depth), depth)
            mf[to, :] = jnp.broadcast_to(jnp.max(best, axis=1, keepdims=True), (depth, LANES))

        sf[...] = jnp.zeros_like(sf)
        acc[...] = jnp.zeros_like(acc)
        at = pl.ds(pl.multiple_of(base, 2 * OWN), 2 * OWN)
        group = 4

        @pl.loop(0, NTGT // group, unroll=2)
        def _(b):
            highs, lows = [], []
            total = sf[...]
            for k in range(group):
                lane = pl.ds(pl.multiple_of((b * group + k) * LANES, LANES), LANES)
                w = jnp.exp2(zf[at, lane] + qg[b * group + k] - mf[...])
                total += w
                high = w.astype(BF16)
                highs.append(high)
                lows.append((w - high.astype(F32)).astype(BF16))
            sf[...] = total
            ys = pl.ds(pl.multiple_of(b * group * LANES, group * LANES), group * LANES)
            both = jnp.dot(jnp.concatenate(highs, axis=1), yf[ys, 0 : 2 * LATENT], preferred_element_type=F32)
            rest = jnp.dot(jnp.concatenate(lows, axis=1), yf[ys, 0:LATENT], preferred_element_type=F32)
            acc[...] += both[:, :LATENT] + both[:, LATENT:] + rest

        for g in range(2):
            rows = slice(g * OWN, (g + 1) * OWN)
            to = chip * 2 + g
            part[to, 0:OWN, :] = acc[rows, :]
            part[to, OWN : OWN + 1, :] = mf[rows, :].T[0:1, :]
            part[to, OWN + 1 : OWN + 2, :] = jnp.sum(sf[rows, :].T, axis=0, keepdims=True)

            def send():
                remote(part.at[to], shares.at[me], part_sem.at[0], part_sem.at[1], (mate(to), t)).start()

            if far == 0:
                pl.when(core != g)(send)
            else:
                send()

    shares[me, 0 : OWN + 2, :] = part[me, 0 : OWN + 2, :]
    wait_bytes(shares.at[pl.ds(0, MATES - 1)], part_sem.at[1])
    tops = [shares[e, OWN : OWN + 1, :] for e in range(MATES)]
    best = tops[0]
    for v in tops[1:]:
        best = jnp.maximum(best, v)
    scales = [jnp.exp2(v - best) for v in tops]
    total = sum(scales[e] * shares[e, OWN + 1 : OWN + 2, :] for e in range(MATES))
    out = jnp.zeros((OWN, LATENT), F32)
    for e in range(MATES):
        out += spread(scales[e] / total) * shares[e, 0:OWN, :]
    out_ref[own_rows, :] = out

    def o_view(chunk, block):
        rows = OWN // O_CHUNKS
        return out_ref.at[pl.ds(pl.multiple_of(block * OWN + chunk * rows, rows), rows), :]

    for distance in range(0, NTGT // 2, 2):
        ring_step(o_view, or_send, or_recv, distance, O_CHUNKS)
    ring_end(o_view, or_recv, O_CHUNKS)

    for chunk in range(2):
        for way in range(2):
            n = reach(way, chunk)
            wait_bytes(tg.at[pl.ds(0, n), pl.ds(0, PIECE // 2), :], tr_send.at[way, chunk])
    for chunk in range(O_CHUNKS):
        for way in range(2):
            wait_bytes(out_ref.at[pl.ds(0, reach(way, chunk) * (OWN // O_CHUNKS)), :], or_send.at[way, chunk])
    wait_bytes(xs.at[pl.ds(0, MATES - 1)], xs_sem.at[0])
    wait_bytes(part.at[pl.ds(0, MATES - 1)], part_sem.at[0])
    for it in range(ITERS):
        wait_bytes(rs.at[it, pl.ds(0, NTGT - 1)], rs_sem.at[it, 0])
        wait_bytes(cr.at[it, pl.ds(0, NSRC - 1)], cr_sem.at[it, 0])
    wait_bytes(qg.at[pl.ds(0, NTGT - 1)], qg_sem.at[0])


def deliver(sp_in, tp_in, bary_in, sp_out, tp_out, bary_out, sp_v, tp_v, bary_v, in_sems, out_sems):
    parts = [(sp_in, sp_v, sp_out), (tp_in, tp_v, tp_out)]
    rows = ROWS // DELIVERIES
    for k in range(DELIVERIES):
        at = pl.ds(k * rows, rows)
        parts.append((bary_in.at[at, :], bary_v.at[at, :], bary_out.at[at, :]))
    ins = [pltpu.make_async_copy(a, v, in_sems.at[k]) for k, (a, v, _) in enumerate(parts)]
    outs = [pltpu.make_async_copy(v, b, out_sems.at[k]) for k, (_, v, b) in enumerate(parts)]
    for copy in ins:
        copy.start()
    for first, second in zip(ins, outs):
        first.wait()
        second.start()
    for copy in outs:
        copy.wait()


def on_device(sources, targets, log_source, log_target):
    vmem = pl.BlockSpec(memory_space=pltpu.VMEM)
    dma = pltpu.SemaphoreType.DMA
    sp, tp, bary = pl.pallas_call(
        kernel,
        out_shape=(
            jax.ShapeDtypeStruct((RCH, LANES), F32),
            jax.ShapeDtypeStruct((CCH, LANES), F32),
            jax.ShapeDtypeStruct((ROWS, LATENT), F32),
        ),
        in_specs=[vmem] * 4,
        out_specs=(vmem,) * 3,
        scratch_shapes=[
            pltpu.VMEM((3 * LATENT, ROWS), BF16),
            pltpu.VMEM((COLS, 3 * LATENT), BF16),
            pltpu.VMEM((COLS, ROWS), F32),
            pltpu.VMEM((MATES * OWN, NTGT * PIECE), F32),
            pltpu.VMEM((COLS, LANES), F32),
            pltpu.VMEM((RCH, LANES), F32),
            pltpu.VMEM((RCH, LANES), F32),
            pltpu.VMEM((CCH, LANES), F32),
            pltpu.VMEM((RCH, 8, LANES), F32),
            pltpu.VMEM((RCH, 8, LANES), F32),
            pltpu.VMEM((COLS, LANES), F32),
            pltpu.VMEM((COLS, LANES), F32),
            pltpu.VMEM((ITERS, RCH, LANES), F32),
            pltpu.VMEM((ITERS, NTGT, RCH, LANES), F32),
            pltpu.VMEM((ITERS, CCH, LANES), F32),
            pltpu.VMEM((ITERS, NSRC, CCH, LANES), F32),
            pltpu.VMEM((CCH, 1, LANES), F32),
            pltpu.VMEM((NTGT, 1, LANES), F32),
            pltpu.VMEM((NTGT, PIECE, LATENT), F32),
            pltpu.VMEM((MATES, OWN, LATENT), F32),
            pltpu.VMEM((MATES * OWN, 3 * LATENT), BF16),
            pltpu.VMEM((NTGT * PIECE, 2 * LATENT), BF16),
            pltpu.VMEM((2 * OWN, LANES), F32),
            pltpu.VMEM((2 * OWN, LANES), F32),
            pltpu.VMEM((2 * OWN, LATENT), F32),
            pltpu.VMEM((MATES, OWN + 8, LATENT), F32),
            pltpu.VMEM((MATES, OWN + 8, LATENT), F32),
            dma((ITERS, 2)),
            dma((ITERS, 2)),
            dma((2,)),
            dma((2, 2)), dma((2, 2, 8)),
            dma((2, O_CHUNKS)), dma((2, O_CHUNKS, 8)),
            dma((2,)),
            dma((2,)),
        ],
        compiler_params=pltpu.CompilerParams(
            collective_id=0, has_side_effects=True, vmem_limit_bytes=56 * 2**20
        ),
        cost_estimate=pl.CostEstimate(flops=6 * 10**9, bytes_accessed=4 * 2**20, transcendentals=10**7),
        name="coupling",
    )(
        sources,
        targets,
        log_source.reshape(RCH, LANES),
        log_target.reshape(CCH, LANES),
    )
    sp, tp, bary = pl.pallas_call(
        deliver,
        out_shape=tuple(jax.ShapeDtypeStruct(v.shape, F32) for v in (sp, tp, bary)),
        in_specs=[pl.BlockSpec(memory_space=pl.ANY)] * 3,
        out_specs=(pl.BlockSpec(memory_space=pl.ANY),) * 3,
        scratch_shapes=[
            pltpu.VMEM((RCH, LANES), F32),
            pltpu.VMEM((CCH, LANES), F32),
            pltpu.VMEM((ROWS, LATENT), F32),
            dma((2 + DELIVERIES,)),
            dma((2 + DELIVERIES,)),
        ],
        name="deliver",
    )(sp, tp, bary)
    return sp.reshape(ROWS), tp.reshape(COLS), bary


def solution(mesh):
    in_specs = (P("src", None), P("tgt", None), P("src"), P("tgt"))
    out_specs = (P("src"), P("tgt"), P("src", None))
    return jax.shard_map(
        on_device, mesh=mesh, in_specs=in_specs, out_specs=out_specs, check_vma=False
    )
```

```python
import functools
import math

import jax
import jax.numpy as jnp
from jax import lax
from jax.experimental import pallas as pl
from jax.experimental.pallas import tpu as pltpu
from jax.sharding import PartitionSpec as P

ITERS = 2
LATENT = 128
LANES = 128
LOG2E = math.log2(math.e)
LN2 = math.log(2.0)
MESH = pl.DeviceIdType.MESH

NSRC, NTGT = 32, 16
GRID_X, GRID_Y = 4, 4
ROWS, COLS = 2048, 1024
RCH, CCH = ROWS // LANES, COLS // LANES
OWN = ROWS // NTGT
O_CHUNKS = 4
MATES = GRID_X * 2
DELIVERIES = 4
PIECE = COLS // MATES
F32, BF16 = jnp.float32, jnp.bfloat16


def split3(v, order, axis=1):
    high = v.astype(BF16)
    low = (v - high.astype(F32)).astype(BF16)
    return jnp.concatenate([(high, low)[k] for k in order], axis=axis)


def dot(a, b):
    return jnp.dot(a, b, preferred_element_type=F32)


def spread(row):
    return jnp.broadcast_to(row, (LANES, LANES)).T


def lse_down(z_ref, b_ref, top_ref, total_ref):
    rows, cols = z_ref.shape
    width, depth = 2, 128

    @pl.loop(0, cols // (width * LANES))
    def _(col):
        def block(n, state):
            at = pl.ds(pl.multiple_of(n * depth, depth), depth)
            out = []
            for k in range(width):
                top, total = state[k]
                lane = pl.multiple_of(col * width * LANES + k * LANES, LANES)
                v = (z_ref[at, pl.ds(lane, LANES)] + b_ref[at, :]).reshape(depth // 8, 8, LANES)
                new = jnp.maximum(top, jnp.max(v, axis=0))
                total = total * jnp.exp2(top - new) + jnp.sum(jnp.exp2(v - new[None]), axis=0)
                out.append((new, total))
            return tuple(out)

        start = (jnp.full((8, LANES), -jnp.inf, F32), jnp.zeros((8, LANES), F32))
        state = lax.fori_loop(0, rows // depth, block, (start,) * width, unroll=True)
        for k in range(width):
            top_ref[col * width + k], total_ref[col * width + k] = state[k]

    tops = top_ref[...]
    best = jnp.max(tops, axis=1)
    total = jnp.sum(total_ref[...] * jnp.exp2(tops - best[:, None, :]), axis=1)
    return best + LOG2E * jnp.log(total)


def lse_across(z_ref, b_ref, top_ref, total_ref, out_ref):
    rows, cols = z_ref.shape
    depth = 16

    @pl.loop(0, rows // depth, unroll=4)
    def _(n):
        at = pl.ds(pl.multiple_of(n * depth, depth), depth)
        v = [z_ref[at, c * LANES : (c + 1) * LANES] + b_ref[c : c + 1, :] for c in range(cols // LANES)]
        top = functools.reduce(jnp.maximum, v)
        top_ref[at, :] = top
        total_ref[at, :] = sum(jnp.exp2(x - top) for x in v)

    for k in range(rows // LANES):
        at = slice(k * LANES, (k + 1) * LANES)
        top = top_ref[at, :].T
        best = jnp.max(top, axis=0, keepdims=True)
        total = jnp.sum(total_ref[at, :].T * jnp.exp2(top - best), axis=0, keepdims=True)
        out_ref[k : k + 1, :] = best + LOG2E * jnp.log(total)


def combine(parts):
    top = jnp.max(parts, axis=0)
    return top + LOG2E * jnp.log(jnp.sum(jnp.exp2(parts - top[None]), axis=0))


def kernel(
    x_ref, y_ref, la_ref, lb_ref, sp_ref, tp_ref, out_ref,
    xt, ya, zt, zf, qb, pv, nx, ny, top8, total8, tops, totals,
    l_row, rs, l_col, cr, qs, qg, tg, xs, xf, yf, mf, sf, acc, part, shares,
    rs_sem, cr_sem, qg_sem, tr_send, tr_recv, or_send, or_recv, xs_sem, part_sem,
):
    s, t = lax.axis_index("src"), lax.axis_index("tgt")
    gx, gy, core = s // (GRID_Y * 2), lax.rem(s // 2, GRID_Y), lax.rem(s, 2)
    me = gx * 2 + core

    def z_peer(k):
        return lax.rem(t + k, NTGT)

    def s_peer(k):
        return lax.rem(s + k, NSRC)

    def mate(e):
        return ((e // 2) * GRID_Y + gy) * 2 + lax.rem(e, 2)

    barrier = pltpu.get_barrier_semaphore()

    @pl.loop(1, NTGT)
    def _(k):
        pl.semaphore_signal(barrier, inc=1, device_id=(s, z_peer(k)), device_id_type=MESH)

    @pl.loop(1, NSRC)
    def _(k):
        pl.semaphore_signal(barrier, inc=1, device_id=(s_peer(k), t), device_id_type=MESH)

    def remote(src, dst, send, recv, device):
        return pltpu.make_async_remote_copy(
            src_ref=src, dst_ref=dst, send_sem=send, recv_sem=recv, device_id=device, device_id_type=MESH
        )

    def wait_bytes(ref, sem):
        remote(ref, ref, sem, sem, (s, t)).wait_recv()

    @pl.loop(0, RCH, unroll=4)
    def _(k):
        at = pl.ds(pl.multiple_of(k * LANES, LANES), LANES)
        xt[:, at] = split3(x_ref[at, :].T * (2.0 * LOG2E), (0, 0, 1), axis=0)

    @pl.loop(0, CCH, unroll=2)
    def _(k):
        at = pl.ds(pl.multiple_of(k * LANES, LANES), LANES)
        y = y_ref[at, :]
        ya[at, :] = split3(y, (0, 1, 0))
        qb[at, :] = jnp.broadcast_to(-LOG2E * jnp.sum(y * y, axis=1, keepdims=True), (LANES, LANES))

    tg[t] = y_ref[pl.ds(pl.multiple_of(me * PIECE, PIECE), PIECE), :]
    own_rows = pl.ds(pl.multiple_of(t * OWN, OWN), OWN)
    xs[me] = x_ref[own_rows, :]

    @pl.loop(0, ROWS // 256)
    def _(k):
        at = pl.ds(pl.multiple_of(k * 256, 256), 256)
        zt[:, at] = dot(ya[...], xt[:, at])

    pl.semaphore_wait(barrier, NTGT - 1 + NSRC - 1)

    def reach(way, chunk):
        return NTGT // 2 - (way ^ chunk % 2)

    def away(way, distance):
        return lax.rem(t + (distance if way == 0 else NTGT - distance), NTGT)

    def ring_wait(view, recv, way, chunk, distance):
        ref = view(chunk, away(1 - way, distance))
        wait_bytes(ref, recv.at[way, chunk, distance - 1])

    def ring_step(view, send, recv, distance, chunks=2):
        for chunk in range(chunks):
            for way in range(2):
                if distance > 0:
                    ring_wait(view, recv, way, chunk, distance)
                ref = view(chunk, away(1 - way, distance))
                for stride in (2, 1):
                    there = distance + stride
                    if there <= reach(way, chunk):
                        at = recv.at[way, chunk, there - 1]
                        remote(ref, ref, send.at[way, chunk], at, (s, away(way, stride))).start()

    def ring_end(view, recv, chunks=2):
        for distance in (1, 3, 5, 7, 8):
            for chunk in range(chunks):
                for way in range(2):
                    if distance <= reach(way, chunk):
                        ring_wait(view, recv, way, chunk, distance)

    def t_view(chunk, block):
        return tg.at[block, pl.ds(chunk * (PIECE // 2), PIECE // 2), :]

    def t_step(step):
        ring_step(t_view, tr_send, tr_recv, step)

    t_step(0)

    @pl.loop(1, MATES)
    def _(k):
        to = mate(lax.rem(me + k, MATES))
        remote(xs.at[me], xs.at[me], xs_sem.at[0], xs_sem.at[1], (to, t)).start()

    def last_scores(first, last):
        @pl.loop(first, last)
        def _(b):
            at = pl.ds(pl.multiple_of(b * 2 * PIECE, 2 * PIECE), 2 * PIECE)
            y = tg[pl.ds(b * 2, 2)].reshape(2 * PIECE, LATENT)
            yf[at, :] = split3(y, (0, 1))
            zf[:, at] = dot(xf[...], split3(y.T, (0, 1, 0), axis=0))

    def last_rows(first, last):
        @pl.loop(first, last)
        def _(e):
            at = pl.ds(pl.multiple_of(e * OWN, OWN), OWN)
            xf[at, :] = split3(xs[e] * (2.0 * LOG2E), (0, 0, 1))

    for it in range(ITERS):
        l_row[it] = lse_down(zt, qb, top8, total8)

        @pl.loop(1, NTGT)
        def _(k):
            remote(l_row.at[it], rs.at[it, t], rs_sem.at[it, 0], rs_sem.at[it, 1], (s, z_peer(k))).start()

        rs[it, t] = l_row[it]
        if it == 0:
            t_step(2)
            for k in range(RCH):
                turned = x_ref[k * LANES : (k + 1) * LANES, :].T
                nx[k : k + 1, :] = jnp.sum(turned * turned, axis=0, keepdims=True)
            for k in range(CCH):
                turned = y_ref[k * LANES : (k + 1) * LANES, :].T
                ny[k : k + 1, :] = jnp.sum(turned * turned, axis=0, keepdims=True)
        else:
            ring_end(t_view, tr_recv)
            last_scores(0, NTGT // 4)

        wait_bytes(rs.at[it, pl.ds(0, NTGT - 1)], rs_sem.at[it, 1])
        row_pot = LOG2E * la_ref[...] - combine(rs[it])
        pv[...] = row_pot
        if it == 0:
            t_step(4)
        lse_across(zt, pv, tops, totals, l_col.at[it])

        @pl.loop(1, NSRC)
        def _(k):
            remote(l_col.at[it], cr.at[it, s], cr_sem.at[it, 0], cr_sem.at[it, 1], (s_peer(k), t)).start()

        cr[it, s] = l_col[it]
        if it == 0:
            wait_bytes(xs.at[pl.ds(0, MATES - 1)], xs_sem.at[1])
            last_rows(0, MATES)
            t_step(6)
        else:
            sp_ref[...] = row_pot * LN2 + nx[...]
            last_scores(NTGT // 4, NTGT // 2)

        wait_bytes(cr.at[it, pl.ds(0, NSRC - 1)], cr_sem.at[it, 1])
        q = LOG2E * lb_ref[...] - combine(cr[it])
        if it == 0:
            for k in range(CCH):
                qb[k * LANES : (k + 1) * LANES, :] = spread(q[k : k + 1, :])

    for k in range(CCH):
        qs[k] = q[k : k + 1, :]
    qg[t] = qs[me]

    @pl.loop(1, NTGT)
    def _(k):
        remote(qs.at[me], qg.at[t], qg_sem.at[0], qg_sem.at[1], (s, z_peer(k))).start()

    tp_ref[...] = q * LN2 + ny[...]
    wait_bytes(qg.at[pl.ds(0, NTGT - 1)], qg_sem.at[1])

    depth = 64
    for far in (2, 1, 3, 0):
        chip = lax.rem(gx + far, GRID_X)
        base = chip * 2 * OWN

        @pl.loop(0, 2 * OWN // depth)
        def _(r):
            at = pl.ds(pl.multiple_of(base + r * depth, depth), depth)
            best = zf[at, 0:LANES] + qg[0]
            for b in range(1, NTGT):
                best = jnp.maximum(best, zf[at, b * LANES : (b + 1) * LANES] + qg[b])
            to = pl.ds(pl.multiple_of(r * depth, depth), depth)
            mf[to, :] = jnp.broadcast_to(jnp.max(best, axis=1, keepdims=True), (depth, LANES))

        sf[...] = jnp.zeros_like(sf)
        acc[...] = jnp.zeros_like(acc)
        at = pl.ds(pl.multiple_of(base, 2 * OWN), 2 * OWN)
        group = 4

        @pl.loop(0, NTGT // group, unroll=2)
        def _(b):
            highs, lows = [], []
            total = sf[...]
            for k in range(group):
                lane = pl.ds(pl.multiple_of((b * group + k) * LANES, LANES), LANES)
                w = jnp.exp2(zf[at, lane] + qg[b * group + k] - mf[...])
                total += w
                high = w.astype(BF16)
                highs.append(high)
                lows.append((w - high.astype(F32)).astype(BF16))
            sf[...] = total
            ys = pl.ds(pl.multiple_of(b * group * LANES, group * LANES), group * LANES)
            both = jnp.dot(jnp.concatenate(highs, axis=1), yf[ys, 0 : 2 * LATENT], preferred_element_type=F32)
            rest = jnp.dot(jnp.concatenate(lows, axis=1), yf[ys, 0:LATENT], preferred_element_type=F32)
            acc[...] += both[:, :LATENT] + both[:, LATENT:] + rest

        for g in range(2):
            rows = slice(g * OWN, (g + 1) * OWN)
            to = chip * 2 + g
            part[to, 0:OWN, :] = acc[rows, :]
            part[to, OWN : OWN + 1, :] = mf[rows, :].T[0:1, :]
            part[to, OWN + 1 : OWN + 2, :] = jnp.sum(sf[rows, :].T, axis=0, keepdims=True)

            def send():
                remote(part.at[to], shares.at[me], part_sem.at[0], part_sem.at[1], (mate(to), t)).start()

            if far == 0:
                pl.when(core != g)(send)
            else:
                send()

    shares[me, 0 : OWN + 2, :] = part[me, 0 : OWN + 2, :]
    wait_bytes(shares.at[pl.ds(0, MATES - 1)], part_sem.at[1])
    tops = [shares[e, OWN : OWN + 1, :] for e in range(MATES)]
    best = tops[0]
    for v in tops[1:]:
        best = jnp.maximum(best, v)
    scales = [jnp.exp2(v - best) for v in tops]
    total = sum(scales[e] * shares[e, OWN + 1 : OWN + 2, :] for e in range(MATES))
    out = jnp.zeros((OWN, LATENT), F32)
    for e in range(MATES):
        out += spread(scales[e] / total) * shares[e, 0:OWN, :]
    out_ref[own_rows, :] = out

    def o_view(chunk, block):
        rows = OWN // O_CHUNKS
        return out_ref.at[pl.ds(pl.multiple_of(block * OWN + chunk * rows, rows), rows), :]

    for distance in range(0, NTGT // 2, 2):
        ring_step(o_view, or_send, or_recv, distance, O_CHUNKS)
    ring_end(o_view, or_recv, O_CHUNKS)

    for chunk in range(2):
        for way in range(2):
            n = reach(way, chunk)
            wait_bytes(tg.at[pl.ds(0, n), pl.ds(0, PIECE // 2), :], tr_send.at[way, chunk])
    for chunk in range(O_CHUNKS):
        for way in range(2):
            wait_bytes(out_ref.at[pl.ds(0, reach(way, chunk) * (OWN // O_CHUNKS)), :], or_send.at[way, chunk])
    wait_bytes(xs.at[pl.ds(0, MATES - 1)], xs_sem.at[0])
    wait_bytes(part.at[pl.ds(0, MATES - 1)], part_sem.at[0])
    for it in range(ITERS):
        wait_bytes(rs.at[it, pl.ds(0, NTGT - 1)], rs_sem.at[it, 0])
        wait_bytes(cr.at[it, pl.ds(0, NSRC - 1)], cr_sem.at[it, 0])
    wait_bytes(qg.at[pl.ds(0, NTGT - 1)], qg_sem.at[0])


def deliver(sp_in, tp_in, bary_in, sp_out, tp_out, bary_out, sp_v, tp_v, bary_v, in_sems, out_sems):
    parts = [(sp_in, sp_v, sp_out), (tp_in, tp_v, tp_out)]
    rows = ROWS // DELIVERIES
    for k in range(DELIVERIES):
        at = pl.ds(k * rows, rows)
        parts.append((bary_in.at[at, :], bary_v.at[at, :], bary_out.at[at, :]))
    ins = [pltpu.make_async_copy(a, v, in_sems.at[k]) for k, (a, v, _) in enumerate(parts)]
    outs = [pltpu.make_async_copy(v, b, out_sems.at[k]) for k, (_, v, b) in enumerate(parts)]
    for copy in ins:
        copy.start()
    for first, second in zip(ins, outs):
        first.wait()
        second.start()
    for copy in outs:
        copy.wait()


def on_device(sources, targets, log_source, log_target):
    vmem = pl.BlockSpec(memory_space=pltpu.VMEM)
    dma = pltpu.SemaphoreType.DMA
    sp, tp, bary = pl.pallas_call(
        kernel,
        out_shape=(
            jax.ShapeDtypeStruct((RCH, LANES), F32),
            jax.ShapeDtypeStruct((CCH, LANES), F32),
            jax.ShapeDtypeStruct((ROWS, LATENT), F32),
        ),
        in_specs=[vmem] * 4,
        out_specs=(vmem,) * 3,
        scratch_shapes=[
            pltpu.VMEM((3 * LATENT, ROWS), BF16),
            pltpu.VMEM((COLS, 3 * LATENT), BF16),
            pltpu.VMEM((COLS, ROWS), F32),
            pltpu.VMEM((MATES * OWN, NTGT * PIECE), F32),
            pltpu.VMEM((COLS, LANES), F32),
            pltpu.VMEM((RCH, LANES), F32),
            pltpu.VMEM((RCH, LANES), F32),
            pltpu.VMEM((CCH, LANES), F32),
            pltpu.VMEM((RCH, 8, LANES), F32),
            pltpu.VMEM((RCH, 8, LANES), F32),
            pltpu.VMEM((COLS, LANES), F32),
            pltpu.VMEM((COLS, LANES), F32),
            pltpu.VMEM((ITERS, RCH, LANES), F32),
            pltpu.VMEM((ITERS, NTGT, RCH, LANES), F32),
            pltpu.VMEM((ITERS, CCH, LANES), F32),
            pltpu.VMEM((ITERS, NSRC, CCH, LANES), F32),
            pltpu.VMEM((CCH, 1, LANES), F32),
            pltpu.VMEM((NTGT, 1, LANES), F32),
            pltpu.VMEM((NTGT, PIECE, LATENT), F32),
            pltpu.VMEM((MATES, OWN, LATENT), F32),
            pltpu.VMEM((MATES * OWN, 3 * LATENT), BF16),
            pltpu.VMEM((NTGT * PIECE, 2 * LATENT), BF16),
            pltpu.VMEM((2 * OWN, LANES), F32),
            pltpu.VMEM((2 * OWN, LANES), F32),
            pltpu.VMEM((2 * OWN, LATENT), F32),
            pltpu.VMEM((MATES, OWN + 8, LATENT), F32),
            pltpu.VMEM((MATES, OWN + 8, LATENT), F32),
            dma((ITERS, 2)),
            dma((ITERS, 2)),
            dma((2,)),
            dma((2, 2)), dma((2, 2, 8)),
            dma((2, O_CHUNKS)), dma((2, O_CHUNKS, 8)),
            dma((2,)),
            dma((2,)),
        ],
        compiler_params=pltpu.CompilerParams(
            collective_id=0, has_side_effects=True, vmem_limit_bytes=56 * 2**20
        ),
        cost_estimate=pl.CostEstimate(flops=6 * 10**9, bytes_accessed=4 * 2**20, transcendentals=10**7),
        name="coupling",
    )(
        sources,
        targets,
        log_source.reshape(RCH, LANES),
        log_target.reshape(CCH, LANES),
    )
    sp, tp, bary = pl.pallas_call(
        deliver,
        out_shape=tuple(jax.ShapeDtypeStruct(v.shape, F32) for v in (sp, tp, bary)),
        in_specs=[pl.BlockSpec(memory_space=pl.ANY)] * 3,
        out_specs=(pl.BlockSpec(memory_space=pl.ANY),) * 3,
        scratch_shapes=[
            pltpu.VMEM((RCH, LANES), F32),
            pltpu.VMEM((CCH, LANES), F32),
            pltpu.VMEM((ROWS, LATENT), F32),
            dma((2 + DELIVERIES,)),
            dma((2 + DELIVERIES,)),
        ],
        name="deliver",
    )(sp, tp, bary)
    return sp.reshape(ROWS), tp.reshape(COLS), bary


def solution(mesh):
    in_specs = (P("src", None), P("tgt", None), P("src"), P("tgt"))
    out_specs = (P("src"), P("tgt"), P("src", None))
    return jax.shard_map(
        on_device, mesh=mesh, in_specs=in_specs, out_specs=out_specs, check_vma=False
    )
```

```python
import functools
import math

import jax
import jax.numpy as jnp
from jax import lax
from jax.experimental import pallas as pl
from jax.experimental.pallas import tpu as pltpu
from jax.sharding import PartitionSpec as P

ITERS = 2
LATENT = 128
LANES = 128
LOG2E = math.log2(math.e)
LN2 = math.log(2.0)
MESH = pl.DeviceIdType.MESH

NSRC, NTGT = 32, 16
GRID_X, GRID_Y = 4, 4
ROWS, COLS = 2048, 1024
RCH, CCH = ROWS // LANES, COLS // LANES
OWN = ROWS // NTGT
O_CHUNKS = 2
MATES = GRID_X * 2
DELIVERIES = 4
PIECE = COLS // MATES
F32, BF16 = jnp.float32, jnp.bfloat16


def split3(v, order, axis=1):
    high = v.astype(BF16)
    low = (v - high.astype(F32)).astype(BF16)
    return jnp.concatenate([(high, low)[k] for k in order], axis=axis)


def dot(a, b):
    return jnp.dot(a, b, preferred_element_type=F32)


def spread(row):
    return jnp.broadcast_to(row, (LANES, LANES)).T


def lse_down(z_ref, b_ref, top_ref, total_ref):
    rows, cols = z_ref.shape
    width, depth = 2, 128

    @pl.loop(0, cols // (width * LANES))
    def _(col):
        def block(n, state):
            at = pl.ds(pl.multiple_of(n * depth, depth), depth)
            out = []
            for k in range(width):
                top, total = state[k]
                lane = pl.multiple_of(col * width * LANES + k * LANES, LANES)
                v = (z_ref[at, pl.ds(lane, LANES)] + b_ref[at, :]).reshape(depth // 8, 8, LANES)
                new = jnp.maximum(top, jnp.max(v, axis=0))
                total = total * jnp.exp2(top - new) + jnp.sum(jnp.exp2(v - new[None]), axis=0)
                out.append((new, total))
            return tuple(out)

        start = (jnp.full((8, LANES), -jnp.inf, F32), jnp.zeros((8, LANES), F32))
        state = lax.fori_loop(0, rows // depth, block, (start,) * width, unroll=True)
        for k in range(width):
            top_ref[col * width + k], total_ref[col * width + k] = state[k]

    tops = top_ref[...]
    best = jnp.max(tops, axis=1)
    total = jnp.sum(total_ref[...] * jnp.exp2(tops - best[:, None, :]), axis=1)
    return best + LOG2E * jnp.log(total)


def lse_across(z_ref, b_ref, top_ref, total_ref, out_ref):
    rows, cols = z_ref.shape
    depth = 16

    @pl.loop(0, rows // depth, unroll=4)
    def _(n):
        at = pl.ds(pl.multiple_of(n * depth, depth), depth)
        v = [z_ref[at, c * LANES : (c + 1) * LANES] + b_ref[c : c + 1, :] for c in range(cols // LANES)]
        top = functools.reduce(jnp.maximum, v)
        top_ref[at, :] = top
        total_ref[at, :] = sum(jnp.exp2(x - top) for x in v)

    for k in range(rows // LANES):
        at = slice(k * LANES, (k + 1) * LANES)
        top = top_ref[at, :].T
        best = jnp.max(top, axis=0, keepdims=True)
        total = jnp.sum(total_ref[at, :].T * jnp.exp2(top - best), axis=0, keepdims=True)
        out_ref[k : k + 1, :] = best + LOG2E * jnp.log(total)


def combine(parts):
    top = jnp.max(parts, axis=0)
    return top + LOG2E * jnp.log(jnp.sum(jnp.exp2(parts - top[None]), axis=0))


def kernel(
    x_ref, y_ref, la_ref, lb_ref, sp_ref, tp_ref, out_ref,
    xt, ya, zt, zf, qb, pv, nx, ny, top8, total8, tops, totals,
    l_row, rs, l_col, cr, qs, qg, tg, xs, xf, yf, mf, sf, wh, wl, part, shares,
    rs_sem, cr_sem, qg_sem, tr_send, tr_recv, or_send, or_recv, xs_sem, part_sem,
):
    s, t = lax.axis_index("src"), lax.axis_index("tgt")
    gx, gy, core = s // (GRID_Y * 2), lax.rem(s // 2, GRID_Y), lax.rem(s, 2)
    me = gx * 2 + core

    def z_peer(k):
        return lax.rem(t + k, NTGT)

    def s_peer(k):
        return lax.rem(s + k, NSRC)

    def mate(e):
        return ((e // 2) * GRID_Y + gy) * 2 + lax.rem(e, 2)

    barrier = pltpu.get_barrier_semaphore()

    @pl.loop(1, NTGT)
    def _(k):
        pl.semaphore_signal(barrier, inc=1, device_id=(s, z_peer(k)), device_id_type=MESH)

    @pl.loop(1, NSRC)
    def _(k):
        pl.semaphore_signal(barrier, inc=1, device_id=(s_peer(k), t), device_id_type=MESH)

    def remote(src, dst, send, recv, device):
        return pltpu.make_async_remote_copy(
            src_ref=src, dst_ref=dst, send_sem=send, recv_sem=recv, device_id=device, device_id_type=MESH
        )

    def wait_bytes(ref, sem):
        remote(ref, ref, sem, sem, (s, t)).wait_recv()

    @pl.loop(0, RCH, unroll=4)
    def _(k):
        at = pl.ds(pl.multiple_of(k * LANES, LANES), LANES)
        xt[:, at] = split3(x_ref[at, :].T * (2.0 * LOG2E), (0, 0, 1), axis=0)

    @pl.loop(0, CCH, unroll=2)
    def _(k):
        at = pl.ds(pl.multiple_of(k * LANES, LANES), LANES)
        y = y_ref[at, :]
        ya[at, :] = split3(y, (0, 1, 0))
        qb[at, :] = jnp.broadcast_to(-LOG2E * jnp.sum(y * y, axis=1, keepdims=True), (LANES, LANES))

    tg[t] = y_ref[pl.ds(pl.multiple_of(me * PIECE, PIECE), PIECE), :]
    own_rows = pl.ds(pl.multiple_of(t * OWN, OWN), OWN)
    xs[me] = x_ref[own_rows, :]

    @pl.loop(0, ROWS // 256)
    def _(k):
        at = pl.ds(pl.multiple_of(k * 256, 256), 256)
        zt[:, at] = dot(ya[...], xt[:, at])

    pl.semaphore_wait(barrier, NTGT - 1 + NSRC - 1)

    def reach(way, chunk):
        return NTGT // 2 - (way ^ chunk % 2)

    def away(way, distance):
        return lax.rem(t + (distance if way == 0 else NTGT - distance), NTGT)

    def ring_wait(view, recv, way, chunk, distance):
        ref = view(chunk, away(1 - way, distance))
        wait_bytes(ref, recv.at[way, chunk, distance - 1])

    def ring_step(view, send, recv, distance, chunks=2):
        for chunk in range(chunks):
            for way in range(2):
                if distance > 0:
                    ring_wait(view, recv, way, chunk, distance)
                ref = view(chunk, away(1 - way, distance))
                for stride in (2, 1):
                    there = distance + stride
                    if there <= reach(way, chunk):
                        at = recv.at[way, chunk, there - 1]
                        remote(ref, ref, send.at[way, chunk], at, (s, away(way, stride))).start()

    def ring_end(view, recv, chunks=2):
        for distance in (1, 3, 5, 7, 8):
            for chunk in range(chunks):
                for way in range(2):
                    if distance <= reach(way, chunk):
                        ring_wait(view, recv, way, chunk, distance)

    def t_view(chunk, block):
        return tg.at[block, pl.ds(chunk * (PIECE // 2), PIECE // 2), :]

    def t_step(step):
        ring_step(t_view, tr_send, tr_recv, step)

    t_step(0)

    @pl.loop(1, MATES)
    def _(k):
        to = mate(lax.rem(me + k, MATES))
        remote(xs.at[me], xs.at[me], xs_sem.at[0], xs_sem.at[1], (to, t)).start()

    def last_scores(first, last):
        @pl.loop(first, last)
        def _(b):
            at = pl.ds(pl.multiple_of(b * 2 * PIECE, 2 * PIECE), 2 * PIECE)
            y = tg[pl.ds(b * 2, 2)].reshape(2 * PIECE, LATENT)
            yf[at, :] = split3(y, (0, 1))
            zf[:, at] = dot(xf[...], split3(y.T, (0, 1, 0), axis=0))

    def last_rows(first, last):
        @pl.loop(first, last)
        def _(e):
            at = pl.ds(pl.multiple_of(e * OWN, OWN), OWN)
            xf[at, :] = split3(xs[e] * (2.0 * LOG2E), (0, 0, 1))

    for it in range(ITERS):
        l_row[it] = lse_down(zt, qb, top8, total8)

        @pl.loop(1, NTGT)
        def _(k):
            remote(l_row.at[it], rs.at[it, t], rs_sem.at[it, 0], rs_sem.at[it, 1], (s, z_peer(k))).start()

        rs[it, t] = l_row[it]
        if it == 0:
            t_step(2)
            for k in range(RCH):
                turned = x_ref[k * LANES : (k + 1) * LANES, :].T
                nx[k : k + 1, :] = jnp.sum(turned * turned, axis=0, keepdims=True)
            for k in range(CCH):
                turned = y_ref[k * LANES : (k + 1) * LANES, :].T
                ny[k : k + 1, :] = jnp.sum(turned * turned, axis=0, keepdims=True)
        else:
            ring_end(t_view, tr_recv)
            last_scores(0, NTGT // 4)

        wait_bytes(rs.at[it, pl.ds(0, NTGT - 1)], rs_sem.at[it, 1])
        row_pot = LOG2E * la_ref[...] - combine(rs[it])
        pv[...] = row_pot
        if it == 0:
            t_step(4)
        lse_across(zt, pv, tops, totals, l_col.at[it])

        @pl.loop(1, NSRC)
        def _(k):
            remote(l_col.at[it], cr.at[it, s], cr_sem.at[it, 0], cr_sem.at[it, 1], (s_peer(k), t)).start()

        cr[it, s] = l_col[it]
        if it == 0:
            wait_bytes(xs.at[pl.ds(0, MATES - 1)], xs_sem.at[1])
            last_rows(0, MATES)
            t_step(6)
        else:
            sp_ref[...] = row_pot * LN2 + nx[...]
            last_scores(NTGT // 4, NTGT // 2)

        wait_bytes(cr.at[it, pl.ds(0, NSRC - 1)], cr_sem.at[it, 1])
        q = LOG2E * lb_ref[...] - combine(cr[it])
        if it == 0:
            for k in range(CCH):
                qb[k * LANES : (k + 1) * LANES, :] = spread(q[k : k + 1, :])

    for k in range(CCH):
        qs[k] = q[k : k + 1, :]
    qg[t] = qs[me]

    @pl.loop(1, NTGT)
    def _(k):
        remote(qs.at[me], qg.at[t], qg_sem.at[0], qg_sem.at[1], (s, z_peer(k))).start()

    tp_ref[...] = q * LN2 + ny[...]
    wait_bytes(qg.at[pl.ds(0, NTGT - 1)], qg_sem.at[1])

    depth = 64
    for far in (2, 1, 3, 0):
        chip = lax.rem(gx + far, GRID_X)
        base = chip * 2 * OWN

        @pl.loop(0, 2 * OWN // depth)
        def _(r):
            at = pl.ds(pl.multiple_of(base + r * depth, depth), depth)
            to = pl.ds(pl.multiple_of(r * depth, depth), depth)
            lanes = [slice(b * LANES, (b + 1) * LANES) for b in range(NTGT)]
            best = functools.reduce(jnp.maximum, [zf[at, lanes[b]] + qg[b] for b in range(NTGT)])
            best = jnp.broadcast_to(jnp.max(best, axis=1, keepdims=True), (depth, LANES))
            total = jnp.zeros((depth, LANES), F32)
            for b in range(NTGT):
                w = jnp.exp2(zf[at, lanes[b]] + qg[b] - best)
                total += w
                high = w.astype(BF16)
                wh[to, lanes[b]] = high
                wl[to, lanes[b]] = (w - high.astype(F32)).astype(BF16)
            mf[to, :] = best
            sf[to, :] = total

        both = dot(wh[...], yf[...])
        sums = both[:, :LATENT] + both[:, LATENT:] + dot(wl[...], yf[:, 0:LATENT])

        for g in range(2):
            rows = slice(g * OWN, (g + 1) * OWN)
            to = chip * 2 + g
            part[to, 0:OWN, :] = sums[rows, :]
            part[to, OWN : OWN + 1, :] = mf[rows, :].T[0:1, :]
            part[to, OWN + 1 : OWN + 2, :] = jnp.sum(sf[rows, :].T, axis=0, keepdims=True)

            def send():
                remote(part.at[to], shares.at[me], part_sem.at[0], part_sem.at[1], (mate(to), t)).start()

            if far == 0:
                pl.when(core != g)(send)
            else:
                send()

    shares[me, 0 : OWN + 2, :] = part[me, 0 : OWN + 2, :]
    wait_bytes(shares.at[pl.ds(0, MATES - 1)], part_sem.at[1])
    tops = [shares[e, OWN : OWN + 1, :] for e in range(MATES)]
    best = tops[0]
    for v in tops[1:]:
        best = jnp.maximum(best, v)
    scales = [jnp.exp2(v - best) for v in tops]
    total = sum(scales[e] * shares[e, OWN + 1 : OWN + 2, :] for e in range(MATES))
    out = jnp.zeros((OWN, LATENT), F32)
    for e in range(MATES):
        out += spread(scales[e] / total) * shares[e, 0:OWN, :]
    out_ref[own_rows, :] = out

    def o_view(chunk, block):
        rows = OWN // O_CHUNKS
        return out_ref.at[pl.ds(pl.multiple_of(block * OWN + chunk * rows, rows), rows), :]

    for distance in range(0, NTGT // 2, 2):
        ring_step(o_view, or_send, or_recv, distance, O_CHUNKS)
    ring_end(o_view, or_recv, O_CHUNKS)

    for chunk in range(2):
        for way in range(2):
            n = reach(way, chunk)
            wait_bytes(tg.at[pl.ds(0, n), pl.ds(0, PIECE // 2), :], tr_send.at[way, chunk])
    for chunk in range(O_CHUNKS):
        for way in range(2):
            wait_bytes(out_ref.at[pl.ds(0, reach(way, chunk) * (OWN // O_CHUNKS)), :], or_send.at[way, chunk])
    wait_bytes(xs.at[pl.ds(0, MATES - 1)], xs_sem.at[0])
    wait_bytes(part.at[pl.ds(0, MATES - 1)], part_sem.at[0])
    for it in range(ITERS):
        wait_bytes(rs.at[it, pl.ds(0, NTGT - 1)], rs_sem.at[it, 0])
        wait_bytes(cr.at[it, pl.ds(0, NSRC - 1)], cr_sem.at[it, 0])
    wait_bytes(qg.at[pl.ds(0, NTGT - 1)], qg_sem.at[0])


def deliver(sp_in, tp_in, bary_in, sp_out, tp_out, bary_out, sp_v, tp_v, bary_v, in_sems, out_sems):
    parts = [(sp_in, sp_v, sp_out), (tp_in, tp_v, tp_out)]
    rows = ROWS // DELIVERIES
    for k in range(DELIVERIES):
        at = pl.ds(k * rows, rows)
        parts.append((bary_in.at[at, :], bary_v.at[at, :], bary_out.at[at, :]))
    ins = [pltpu.make_async_copy(a, v, in_sems.at[k]) for k, (a, v, _) in enumerate(parts)]
    outs = [pltpu.make_async_copy(v, b, out_sems.at[k]) for k, (_, v, b) in enumerate(parts)]
    for copy in ins:
        copy.start()
    for first, second in zip(ins, outs):
        first.wait()
        second.start()
    for copy in outs:
        copy.wait()


def on_device(sources, targets, log_source, log_target):
    vmem = pl.BlockSpec(memory_space=pltpu.VMEM)
    dma = pltpu.SemaphoreType.DMA
    sp, tp, bary = pl.pallas_call(
        kernel,
        out_shape=(
            jax.ShapeDtypeStruct((RCH, LANES), F32),
            jax.ShapeDtypeStruct((CCH, LANES), F32),
            jax.ShapeDtypeStruct((ROWS, LATENT), F32),
        ),
        in_specs=[vmem] * 4,
        out_specs=(vmem,) * 3,
        scratch_shapes=[
            pltpu.VMEM((3 * LATENT, ROWS), BF16),
            pltpu.VMEM((COLS, 3 * LATENT), BF16),
            pltpu.VMEM((COLS, ROWS), F32),
            pltpu.VMEM((MATES * OWN, NTGT * PIECE), F32),
            pltpu.VMEM((COLS, LANES), F32),
            pltpu.VMEM((RCH, LANES), F32),
            pltpu.VMEM((RCH, LANES), F32),
            pltpu.VMEM((CCH, LANES), F32),
            pltpu.VMEM((RCH, 8, LANES), F32),
            pltpu.VMEM((RCH, 8, LANES), F32),
            pltpu.VMEM((COLS, LANES), F32),
            pltpu.VMEM((COLS, LANES), F32),
            pltpu.VMEM((ITERS, RCH, LANES), F32),
            pltpu.VMEM((ITERS, NTGT, RCH, LANES), F32),
            pltpu.VMEM((ITERS, CCH, LANES), F32),
            pltpu.VMEM((ITERS, NSRC, CCH, LANES), F32),
            pltpu.VMEM((CCH, 1, LANES), F32),
            pltpu.VMEM((NTGT, 1, LANES), F32),
            pltpu.VMEM((NTGT, PIECE, LATENT), F32),
            pltpu.VMEM((MATES, OWN, LATENT), F32),
            pltpu.VMEM((MATES * OWN, 3 * LATENT), BF16),
            pltpu.VMEM((NTGT * PIECE, 2 * LATENT), BF16),
            pltpu.VMEM((2 * OWN, LANES), F32),
            pltpu.VMEM((2 * OWN, LANES), F32),
            pltpu.VMEM((2 * OWN, NTGT * PIECE), BF16),
            pltpu.VMEM((2 * OWN, NTGT * PIECE), BF16),
            pltpu.VMEM((MATES, OWN + 8, LATENT), F32),
            pltpu.VMEM((MATES, OWN + 8, LATENT), F32),
            dma((ITERS, 2)),
            dma((ITERS, 2)),
            dma((2,)),
            dma((2, 2)), dma((2, 2, 8)),
            dma((2, O_CHUNKS)), dma((2, O_CHUNKS, 8)),
            dma((2,)),
            dma((2,)),
        ],
        compiler_params=pltpu.CompilerParams(
            collective_id=0, has_side_effects=True, vmem_limit_bytes=56 * 2**20
        ),
        cost_estimate=pl.CostEstimate(flops=6 * 10**9, bytes_accessed=4 * 2**20, transcendentals=10**7),
        name="coupling",
    )(
        sources,
        targets,
        log_source.reshape(RCH, LANES),
        log_target.reshape(CCH, LANES),
    )
    sp, tp, bary = pl.pallas_call(
        deliver,
        out_shape=tuple(jax.ShapeDtypeStruct(v.shape, F32) for v in (sp, tp, bary)),
        in_specs=[pl.BlockSpec(memory_space=pl.ANY)] * 3,
        out_specs=(pl.BlockSpec(memory_space=pl.ANY),) * 3,
        scratch_shapes=[
            pltpu.VMEM((RCH, LANES), F32),
            pltpu.VMEM((CCH, LANES), F32),
            pltpu.VMEM((ROWS, LATENT), F32),
            dma((2 + DELIVERIES,)),
            dma((2 + DELIVERIES,)),
        ],
        name="deliver",
    )(sp, tp, bary)
    return sp.reshape(ROWS), tp.reshape(COLS), bary


def solution(mesh):
    in_specs = (P("src", None), P("tgt", None), P("src"), P("tgt"))
    out_specs = (P("src"), P("tgt"), P("src", None))
    return jax.shard_map(
        on_device, mesh=mesh, in_specs=in_specs, out_specs=out_specs, check_vma=False
    )
```
